256 devices in a mesh: ctx: 32 (over x, z), head: 8 (over y, core).
Axes of the slice: x: 4, y: 4, z: 8, core: 2. Of those that a mesh axis runs over, the one named last changes fastest.
Arguments:
- queries: bfloat16 [8192, 2048], P('ctx', 'head'), may hold values from -24 to 24
- key_rows: bfloat16 [8192, 2048], P('ctx', 'head'), may hold values from -24 to 24
- value_rows: bfloat16 [8192, 2048], P('ctx', 'head'), may hold values from -6 to 6
- w_out: bfloat16 [2048, 2048], P('head'), may hold values from -0.125 to 0.125
- out_grad: bfloat16 [8192, 2048], P('ctx', 'head'), may hold values from -6 to 6
- tile_kind: int32 [64, 64], replicated, may hold values from 0 to 2, as said below
Outputs:
- layer_out: bfloat16 [8192, 2048], P('ctx', 'head')
- query_grad: bfloat16 [8192, 2048], P('ctx', 'head')
- key_grad: bfloat16 [8192, 2048], P('ctx', 'head')
- value_grad: bfloat16 [8192, 2048], P('ctx', 'head')
- weight_grad: bfloat16 [2048, 2048], P('head', 'ctx')
The draws below stay inside these ranges and needn't reach their ends.
Inputs may be any that keep to these rules, and one draw needn't show every extreme that they name: `tile_kind`: entry [b, c] is the kind of the tile of query block b and key block c: 0 the tile is skipped, 1 every query of block b sees every key of block c, 2 query i sees key j only where j % 128 <= i % 128. Every diagonal entry is 2. A key block is needed by an index of ctx where some of that index's 2 query blocks has a nonzero entry for it; from the key blocks of any other index of ctx an index needs at most 1, and in every draw some index needs exactly 1 from every other index.
All inputs are finite; a program needn't handle non-finite values.
Results may differ from the reference program's by a relative error of at most 0.034.
Values may be sent and summed in bfloat16 or wider, within the bound.
A program may use at most 64 MiB of HBM per device.

```python
import jax
import jax.numpy as jnp
from jax import lax

HEADS = 16
HD = 128
D = 2048
TILE_TOKENS = 128
KB_DEV = 2
KEY_BLOCK_LIMIT = 1
TOK_DEV = 256
NB = 64
TOKENS = 8192
N_CTX = 32


def drawn_rows(key):
    return jnp.clip(jax.random.normal(jax.random.fold_in(key, 3), (TOKENS, D), jnp.float32), -4.0, 4.0)


def draw_queries(key, part):
    key = jax.random.fold_in(key, 11)
    result = drawn_rows(key)
    return result.astype(jnp.bfloat16)


def draw_key_rows(key, part):
    key = jax.random.fold_in(key, 23)
    result = drawn_rows(key)
    return result.astype(jnp.bfloat16)


def draw_tile_kind(key, part):
    key = jax.random.fold_in(key, 37)
    device_list = NB // KB_DEV
    keys = [jax.random.fold_in(key, index) for index in range(9)]
    heavy = jax.random.randint(keys[0], (device_list,), 0, 4)
    forced_dev = jax.random.randint(keys[1], (), 0, device_list)
    heavy = jnp.where(jnp.arange(device_list) == forced_dev, 3, heavy)
    rolls = jax.random.randint(keys[2], (device_list, device_list), 0, 8)
    flags = rolls < 2 + 2 * heavy[:, None]
    counts = jnp.where(flags, jax.random.randint(keys[3], (device_list, device_list), 1, KEY_BLOCK_LIMIT + 1), 0)
    counts = jnp.where(heavy[:, None] == 3, KEY_BLOCK_LIMIT, counts)
    offsets = jax.random.randint(keys[4], (device_list, device_list), 0, KB_DEV)
    chooser = jax.random.randint(keys[5], (device_list, device_list), 0, KB_DEV)
    query_block = jnp.arange(NB)[:, None]
    key_block = jnp.arange(NB)[None, :]
    query_dev = query_block // KB_DEV
    key_dev = key_block // KB_DEV
    key_slot = key_block % KB_DEV
    query_slot = query_block % KB_DEV
    needed = (key_slot - offsets[query_dev, key_dev]) % KB_DEV < counts[query_dev, key_dev]
    same_dev = query_dev == key_dev
    needed = needed | same_dev
    any_kind = jax.random.randint(keys[6], (NB, NB), 0, 3)
    forced_kind = jax.random.randint(keys[7], (NB, NB), 1, 3)
    designated = (query_slot == chooser[query_dev, key_dev]) & jnp.logical_not(same_dev)
    kinds = jnp.where(needed, jnp.where(designated, forced_kind, any_kind), 0)
    kinds = jnp.where(query_block == key_block, 2, kinds)
    return kinds.astype(jnp.int32)


def steps_of(rng, shape, split, low, largest):
    gain, own = 1.0, jax.random.fold_in(rng, 6)
    for axis_at, parts in split:
        draws = jnp.exp(jax.random.uniform(jax.random.fold_in(own, axis_at), (parts,), jnp.float32, low / len(split), largest / len(split)))
        gain = gain * jnp.repeat(draws, shape[axis_at] // parts).reshape([-1 if axis == axis_at else 1 for axis in range(len(shape))])
    return gain


def normal_values(stream_key, shape, scale, bound, pieces=(), held_as=jnp.bfloat16):
    drawn = scale * jax.random.normal(stream_key, shape, jnp.float32)
    if pieces:
        drawn = drawn * steps_of(stream_key, shape, pieces, -0.22, 0.18)
    return jnp.clip(drawn, -bound, bound).astype(held_as)


def setup_inputs(seed: int = 0) -> dict:
    arg_keys = jax.random.split(jax.random.key(seed), 7)
    queries = draw_queries(jax.random.fold_in(arg_keys[6], 71), 0)
    key_rows = draw_key_rows(jax.random.fold_in(arg_keys[6], 71), 0)
    value_rows = normal_values(arg_keys[2], (TOKENS, D), 1.0, 6.0, ((0, 32), (1, 8)))
    w_out = normal_values(arg_keys[3], (D, D), D ** -0.5, 0.125, ((0, 8),))
    out_grad = normal_values(arg_keys[4], (TOKENS, D), 1.0, 6.0, ((0, 32), (1, 8)))
    tile_kind = draw_tile_kind(jax.random.fold_in(arg_keys[6], 71), 0)
    return {"queries": queries, "key_rows": key_rows, "value_rows": value_rows, "w_out": w_out, "out_grad": out_grad, "tile_kind": tile_kind}


def allowed_rows(tile_kind, stretch, tokens):
    kinds = lax.dynamic_slice_in_dim(tile_kind, (stretch * KB_DEV).astype(jnp.int32), KB_DEV, 0)
    blocks = tile_kind.shape[1]
    spread = jnp.broadcast_to(kinds[:, None, :, None], (KB_DEV, TILE_TOKENS, blocks, TILE_TOKENS)).reshape(TOK_DEV, tokens)
    query_pos = jnp.arange(TOK_DEV, dtype=jnp.int32) % TILE_TOKENS
    key_pos = jnp.arange(tokens, dtype=jnp.int32) % TILE_TOKENS
    lower = query_pos[:, None] >= key_pos[None, :]
    return (spread == 1) | ((spread == 2) & lower)


def masked_scores(query_part, key_head, tile_kind, stretch):
    tokens = key_head.shape[0]
    raw = jnp.dot(query_part, key_head.T, preferred_element_type=jnp.float32) * (HD ** -0.5)
    return jnp.where(allowed_rows(tile_kind, stretch, tokens), raw, -jnp.inf)


def reference(queries, key_rows, value_rows, w_out, out_grad, tile_kind):
    tokens = queries.shape[0]

    def heads_first(array):
        return array.reshape(tokens, HEADS, HD).transpose(1, 0, 2)

    def heads_last(array):
        return array.transpose(1, 0, 2).reshape(tokens, HEADS * HD)

    q_heads = heads_first(queries)
    k_heads = heads_first(key_rows)
    v_heads = heads_first(value_rows)
    stretches = jnp.arange(N_CTX, dtype=jnp.int32)

    def forward_head(inputs):
        query_head, key_head, value_head = inputs

        def per_stretch(stretch):
            query_part = lax.dynamic_slice_in_dim(query_head, stretch * TOK_DEV, TOK_DEV, 0)
            scores = masked_scores(query_part, key_head, tile_kind, stretch)
            row_max = jnp.max(scores, axis=1)
            log_total = row_max + jnp.log(jnp.sum(jnp.exp(scores - row_max[:, None]), axis=1))
            probs = jnp.exp(scores - log_total[:, None]).astype(jnp.bfloat16)
            result = jnp.dot(probs, value_head, preferred_element_type=jnp.float32).astype(jnp.bfloat16)
            return result, log_total

        results, totals = lax.map(per_stretch, stretches)
        return results.reshape(tokens, HD), totals.reshape(tokens)

    attn_heads, log_heads = lax.map(forward_head, (q_heads, k_heads, v_heads))
    attn = heads_last(attn_heads)
    layer_out = jnp.dot(attn, w_out, preferred_element_type=jnp.float32).astype(jnp.bfloat16)
    d_attn = jnp.dot(out_grad, w_out.T, preferred_element_type=jnp.float32).astype(jnp.bfloat16)
    weight_grad = jnp.dot(attn.T, out_grad, preferred_element_type=jnp.float32).astype(jnp.bfloat16)
    grad_heads = heads_first(d_attn)
    delta = jnp.sum(grad_heads.astype(jnp.float32) * attn_heads.astype(jnp.float32), axis=2)

    def backward_head(inputs):
        query_head, key_head, value_head, grad_head, log_head, delta_head = inputs

        def per_stretch(carry, stretch):
            key_total, value_total = carry
            start = stretch * TOK_DEV
            query_part = lax.dynamic_slice_in_dim(query_head, start, TOK_DEV, 0)
            grad_part = lax.dynamic_slice_in_dim(grad_head, start, TOK_DEV, 0)
            log_part = lax.dynamic_slice_in_dim(log_head, start, TOK_DEV, 0)
            delta_part = lax.dynamic_slice_in_dim(delta_head, start, TOK_DEV, 0)
            scores = masked_scores(query_part, key_head, tile_kind, stretch)
            probs = jnp.exp(scores - log_part[:, None])
            dprobs = jnp.dot(grad_part, value_head.T, preferred_element_type=jnp.float32)
            dscores = (probs * (dprobs - delta_part[:, None]) * (HD ** -0.5)).astype(jnp.bfloat16)
            query_term = jnp.dot(dscores, key_head, preferred_element_type=jnp.float32).astype(jnp.bfloat16)
            key_term = jnp.dot(dscores.T, query_part, preferred_element_type=jnp.float32).astype(jnp.bfloat16)
            value_term = jnp.dot(probs.astype(jnp.bfloat16).T, grad_part, preferred_element_type=jnp.float32).astype(jnp.bfloat16)
            key_term, value_term = lax.optimization_barrier((key_term, value_term))
            return (key_total + key_term.astype(jnp.float32), value_total + value_term.astype(jnp.float32)), query_term

        empty = jnp.zeros((tokens, HD), jnp.float32)
        (key_total, value_total), query_terms = lax.scan(per_stretch, (empty, empty), stretches)
        return query_terms.reshape(tokens, HD), key_total.astype(jnp.bfloat16), value_total.astype(jnp.bfloat16)

    query_heads_grad, key_heads_grad, value_heads_grad = lax.map(
        backward_head, (q_heads, k_heads, v_heads, grad_heads, log_heads, delta))
    return layer_out, heads_last(query_heads_grad), heads_last(key_heads_grad), heads_last(value_heads_grad), weight_grad
```

```python
import functools

import jax
import jax.numpy as jnp
from jax import lax
from jax.experimental import pallas as pl
from jax.experimental.pallas import tpu as pltpu
from jax.sharding import PartitionSpec as P

HD = 128
TILE = 128
NX, NY, NZ = 4, 4, 8
TOK = 256
HALF = 512
SCALE = HD ** -0.5
EXP2_SCALE = SCALE * 1.4426950408889634
NEG = -1e30
MESH = pl.DeviceIdType.MESH
BF = jnp.bfloat16
F32 = jnp.float32
NT = (((1,), (1,)), ((), ()))
NN = (((1,), (0,)), ((), ()))
TN = (((0,), (0,)), ((), ()))


def dot(a, b, dims):
    return lax.dot_general(a, b, dims, preferred_element_type=F32)


def kernel(
    q_ref, k_ref, v_ref, w_ref, g_ref, kind_ref,
    out_ref, dq_ref, dk_ref, dv_ref, wg_ref,
    kv, qs, dos, pst, mst, oT, dqT, mrow, lrow, aT, dof,
    g_all, w_all, dsend, gx, osend, afull, aall,
    part, sib_out, sib_in, rs_out, rs_in, wg_out, wg_in, gsend, gin,
    a_send, a_recv, ag_send, ag_recv, sib_send, sib_recv,
    y_send, y_recv, yf_send, yf_recv, w_send, w_recv, d_send, d_recv, gx_send, gx_recv,
    o_send, o_recv, ya_send, ya_recv, yaf_send, yaf_recv,
    rs_send, rs_recv, sb_send, sb_recv, wz_send, wz_recv, f_send, f_recv,
):
    i = lax.axis_index("ctx")
    j = lax.axis_index("head")
    x, z = i // NZ, i % NZ
    y, c = j // 2, j % 2
    xc, xr = x // 2, x % 2

    def dev(x_, z_, y_, c_):
        return (x_ * NZ + z_, y_ * 2 + c_)

    sibling = dev(x, z, y, 1 - c)

    def remote(src, dst, ss, rs, to):
        return pltpu.make_async_remote_copy(
            src_ref=src, dst_ref=dst, send_sem=ss, recv_sem=rs, device_id=to, device_id_type=MESH
        )

    def await_at(dst, sem):
        pltpu.make_async_copy(dst, dst, sem).wait()

    barrier = pltpu.get_barrier_semaphore()
    partners = []
    for dx in range(NX):
        for dc in range(2):
            if dx or dc:
                partners.append(dev((x + dx) % NX, z, y, (c + dc) % 2))
    for dy in range(1, NY):
        for dc in range(2):
            partners.append(dev(x, z, (y + dy) % NY, (c + dc) % 2))
    for dz in range(1, NZ):
        partners.append(dev(x, (z + dz) % NZ, y, c))
    for to in partners:
        pl.semaphore_signal(barrier, inc=1, device_id=to, device_id_type=MESH)
    pl.semaphore_wait(barrier, len(partners))

    my_rows = pl.ds(pl.multiple_of(x * TOK, TOK), TOK)
    q_rows = pl.ds(pl.multiple_of(xr * TOK, TOK), TOK)
    half_rows = pl.ds(pl.multiple_of(c * HALF, HALF), HALF)

    def a_dst(a):
        if a == 2:
            return qs.at[q_rows, :]
        return kv.at[z, a, my_rows, :]

    def a_copies(e, a):
        src = (k_ref, v_ref, q_ref)[a].at[:, pl.ds(e * HD, HD)]
        far = remote(src, a_dst(a), a_send.at[e, a], a_recv.at[xr, a], dev(2 * c + e, z, y, xc))
        near = pltpu.make_async_copy(src, a_dst(a), a_recv.at[xr, a])
        return far, near

    for a in range(3):
        for e in range(2):
            far, near = a_copies(e, a)
            pl.when(x != 2 * c + e)(far.start)
            pl.when(x == 2 * c + e)(near.start)

    def y_copies(k, src, dst, ss, rs):
        if k == 0:
            return remote(src, dst.at[j], ss.at[0], rs.at[0], sibling)
        return remote(src, dst.at[j], ss.at[k], rs.at[k], dev(x, z, (y + k) % NY, c))

    def y_slot(k, core):
        return ((y - k) % NY) * 2 + core

    def y_forward(k, dst, ss, rs):
        slot = y_slot(k, c)
        return remote(dst.at[slot], dst.at[slot], ss.at[k], rs.at[k], sibling)

    for k in (1, 2, 3, 0):
        y_copies(k, g_ref, g_all, y_send, y_recv).start()
    g_all[j] = g_ref[...]
    w_all[j] = w_ref[:, pl.ds(pl.multiple_of(j * TOK, TOK), TOK)]

    def w_copy(k):
        to = (j + k) % 8
        return remote(
            w_ref.at[:, pl.ds(pl.multiple_of(to * TOK, TOK), TOK)], w_all.at[j],
            w_send.at[k], w_recv.at[k], (i, to),
        )

    def w_wait(k):
        await_at(w_all.at[(j - k) % 8], w_recv.at[k])

    def ag_copy(direction, dist, a, zs):
        ref = kv.at[zs, a, half_rows, :]
        step = 1 - 2 * direction
        return remote(
            ref, ref, ag_send.at[direction, dist - 1, a], ag_recv.at[direction, dist - 1, a],
            dev(x, (z + step) % NZ, y, c),
        )

    def sib_copy(t, a, zs):
        ref = kv.at[zs, a, half_rows, :]
        return remote(ref, ref, sib_send.at[t, a], sib_recv.at[t, a], sibling)

    kpos = lax.broadcasted_iota(jnp.int32, (TILE, HALF), 0)
    qpos = lax.broadcasted_iota(jnp.int32, (TILE, HALF), 1) % TILE
    diff = kpos - qpos

    def block_of(half, b, zs):
        return 2 * ((2 * half + b // 2) * NZ + zs) + b % 2

    def forward_unit(zs, half):
        rows = pl.ds(pl.multiple_of(half * HALF, HALF), HALF)
        s = dot(kv[zs, 0, rows, :], qs[...], NT)
        parts = []
        for kb in range(4):
            limits = []
            for qb in range(4):
                kind = kind_ref[block_of(c, qb, z), block_of(half, kb, zs)]
                limit = jnp.where(kind == 1, 1000, jnp.where(kind == 2, 0, -1000))
                limits.append(jnp.full((1, TILE), limit, jnp.int32))
            limit = jnp.concatenate(limits, axis=1)
            parts.append(jnp.where(diff <= limit, s[kb * TILE:(kb + 1) * TILE, :], NEG))
        s = jnp.concatenate(parts, axis=0)
        old = mrow[...]
        new = jnp.maximum(old, jnp.max(s, axis=0, keepdims=True))
        alpha = jnp.exp2((old - new) * EXP2_SCALE)
        p = jnp.exp2((s - new) * EXP2_SCALE)
        lrow[...] = lrow[...] * alpha + jnp.sum(p, axis=0, keepdims=True)
        mrow[...] = new
        mst[zs, half] = new
        pb = p.astype(BF)
        pst[zs, half] = pb
        oT[...] = oT[...] * alpha + dot(kv[zs, 1, rows, :].T, pb, NN)

    mrow[...] = jnp.full(mrow.shape, NEG, F32)
    lrow[...] = jnp.zeros(lrow.shape, F32)
    oT[...] = jnp.zeros(oT.shape, F32)

    def d_copies(e):
        src = dsend.at[:, pl.ds(e * HD, HD)]
        dst = dos.at[q_rows, :]
        far = remote(src, dst, d_send.at[e], d_recv.at[xr], dev(2 * c + e, z, y, xc))
        near = pltpu.make_async_copy(src, dst, d_recv.at[xr])
        return far, near

    def gx_copy(k):
        to = (x + k) % NX
        return remote(
            g_all.at[pl.ds(2 * to, 2)], gx.at[x], gx_send.at[k], gx_recv.at[k], dev(to, z, y, c)
        )

    def forward_step(t, carry):
        dist = (t + 1) // 2
        odd = t % 2
        zs = (z + dist * (1 - 2 * odd)) % NZ

        @pl.when(t == 0)
        def _():
            for a in range(2):
                for r in range(2):
                    await_at(kv.at[z, a, pl.ds(r * TOK, TOK), :], a_recv.at[r, a])
                for direction in range(2):
                    ag_copy(direction, 1, a, z).start()
                sib_copy(t, a, z).start()
            for r in range(2):
                await_at(qs.at[pl.ds(r * TOK, TOK), :], a_recv.at[r, 2])

        @pl.when((odd == 1) & (t < 7))
        def _():
            for a in range(2):
                for direction in range(2):
                    src = (z + dist * (2 * direction - 1)) % NZ
                    await_at(kv.at[src, a, half_rows, :], ag_recv.at[direction, dist - 1, a])
                    forward = ag_copy(direction, dist + 1, a, src)
                    if direction == a:
                        forward.start()
                    else:
                        pl.when(dist < 3)(forward.start)
                    sib_copy(t + direction, a, src).start()

        @pl.when(t == 7)
        def _():
            for a in range(2):
                await_at(kv.at[zs, a, half_rows, :], ag_recv.at[a, 3, a])
                sib_copy(t, a, zs).start()

        @pl.when(t == 4)
        def _():
            for k in (1, 2, 3):
                await_at(g_all.at[y_slot(k, c)], y_recv.at[k])
                y_forward(k, g_all, yf_send, yf_recv).start()

        @pl.when(t == 5)
        def _():
            await_at(g_all.at[y * 2 + 1 - c], y_recv.at[0])
            for k in (1, 2, 3):
                await_at(g_all.at[y_slot(k, 1 - c)], yf_recv.at[k])
            d = jnp.zeros((TOK, TOK), F32)
            for h in range(8):
                d = d + dot(g_all[h], w_ref[:, h * TOK:(h + 1) * TOK], NT)
            dsend[...] = d.astype(BF)
            for e in range(2):
                far, near = d_copies(e)
                pl.when(x != 2 * c + e)(far.start)
                pl.when(x == 2 * c + e)(near.start)
            for k in range(1, NX):
                gx_copy(k).start()
            for h in range(2):
                gx[x, h] = g_all[2 * x + h]
            for k in range(1, 8):
                w_copy(k).start()

        forward_unit(zs, c)
        for a in range(2):
            other = pl.ds(pl.multiple_of((1 - c) * HALF, HALF), HALF)
            await_at(kv.at[zs, a, other, :], sib_recv.at[t, a])
        forward_unit(zs, 1 - c)
        return carry

    lax.fori_loop(0, 8, forward_step, 0)

    inv = 1.0 / lrow[...]
    attnT = (oT[...] * inv).astype(BF).astype(F32)
    aT[...] = attnT
    osend[...] = attnT.T.astype(BF)

    def o_copies(k):
        to = (x + k) % NX
        dst = afull.at[c, :, pl.ds(pl.multiple_of(xr * HD, HD), HD)]
        far = remote(osend, dst, o_send.at[k], o_recv.at[xr, c], dev(to, z, y, xc))
        near = pltpu.make_async_copy(osend, dst, o_recv.at[xr, c])
        return far, near

    for k in range(NX):
        far, near = o_copies(k)
        if k:
            far.start()
        else:
            pl.when(c != xc)(far.start)
            pl.when(c == xc)(near.start)

    for r in range(2):
        await_at(dos.at[pl.ds(r * TOK, TOK), :], d_recv.at[r])
    dof[...] = dos[...].astype(F32).T
    dqT[...] = jnp.zeros(dqT.shape, F32)
    for a in range(2):
        rs_in[a, 3, 1 - a] = jnp.zeros((HALF, HD), BF)

    def sb_copy(u):
        return remote(sib_out.at[u], sib_in.at[u], sb_send.at[u], sb_recv.at[u], sibling)

    def rs_copy(direction, dist, a):
        step = 1 - 2 * direction
        return remote(
            rs_out.at[direction, dist - 1, a], rs_in.at[direction, dist - 1, a],
            rs_send.at[direction, dist - 1, a], rs_recv.at[direction, dist - 1, a],
            dev(x, (z + step) % NZ, y, c),
        )

    def backward_unit(zs, half):
        rows = pl.ds(pl.multiple_of(half * HALF, HALF), HALF)
        factor = jnp.exp2((mst[zs, half] - mrow[...]) * EXP2_SCALE) / lrow[...]
        dob = (dof[...] * factor).astype(BF)
        delta = jnp.sum(dob.astype(F32) * aT[...], axis=0, keepdims=True)
        p = pst[zs, half]
        dv = dot(p, dob, NT)
        dp = dot(kv[zs, 1, rows, :], dob, NN)
        ds = (p.astype(F32) * (dp - delta)).astype(BF)
        dk = dot(ds, qs[...], NN) * SCALE
        dqT[...] += dot(kv[zs, 0, rows, :].T, ds, NN)
        return dk, dv

    def attn_parts_wait():
        for e in range(2):
            for half in range(2):
                await_at(afull.at[half, :, pl.ds(e * HD, HD)], o_recv.at[e, half])

    own_attn = afull.at[xc, q_rows, :]

    def wz_copy(k):
        to = (z + k) % NZ
        return remote(
            wg_out.at[to], wg_in.at[z], wz_send.at[k], wz_recv.at[k], dev(x, to, y, c)
        )

    def backward_step(u, carry):
        dist = (8 - u) // 2
        odd = u % 2
        zs = (z + dist * (2 * odd - 1)) % NZ
        dk, dv = backward_unit(zs, 1 - c)
        sib_out[u, 0] = dk.astype(BF)
        sib_out[u, 1] = dv.astype(BF)
        sb_copy(u).start()
        dk, dv = backward_unit(zs, c)
        part[u, 0] = dk
        part[u, 1] = dv

        def total(v, a):
            return part[v, a] + sib_in[v, a].astype(F32)

        @pl.when(u == 0)
        def _():
            await_at(sib_in.at[u], sb_recv.at[u])
            for a in range(2):
                rs_out[a, 3, a] = total(u, a).astype(BF)
                rs_copy(a, 4, a).start()

        @pl.when((u > 0) & (odd == 0))
        def _():
            for direction in range(2):
                await_at(sib_in.at[u - 1 + direction], sb_recv.at[u - 1 + direction])
            for a in range(2):
                for direction in range(2):
                    incoming = rs_in.at[direction, dist, a]
                    if a == direction:
                        await_at(incoming, rs_recv.at[direction, dist, a])
                    else:
                        @pl.when(dist < 3)
                        def _():
                            await_at(incoming, rs_recv.at[direction, dist, a])
                    value = total(u - 1 + direction, a) + incoming[...].astype(F32)
                    rs_out[direction, dist - 1, a] = value.astype(BF)
                    rs_copy(direction, dist, a).start()

        @pl.when(u == 4)
        def _():
            attn_parts_wait()
            for k in (1, 2, 3, 0):
                y_copies(k, own_attn, aall, ya_send, ya_recv).start()
            aall[j] = own_attn[...]
            for h in range(2):
                wg = jnp.zeros((TOK, TOK), F32)
                for xx in range(NX):
                    if h == 0 and xx > 0:
                        await_at(gx.at[(x - xx) % NX], gx_recv.at[xx])
                for xx in range(NX):
                    at = afull[xx // 2, (xx % 2) * TOK:(xx % 2 + 1) * TOK, :]
                    wg = wg + dot(gx[xx, h], at, TN)
                wg = wg.astype(BF)
                for n in range(4):
                    wg_out[4 * h + n] = wg[n * 64:(n + 1) * 64, :]
            for k in range(1, NZ):
                wz_copy(k).start()
            wg_in[z] = wg_out[z]

        @pl.when(u == 6)
        def _():
            for k in (1, 2, 3):
                await_at(aall.at[y_slot(k, c)], ya_recv.at[k])
                y_forward(k, aall, yaf_send, yaf_recv).start()

        return carry

    lax.fori_loop(0, 8, backward_step, 0)

    def f_copies(r, a):
        src = gsend.at[a, pl.ds(r * TOK, TOK), :]
        dst = gin.at[xr, a]
        far = remote(src, dst, f_send.at[r, a], f_recv.at[xr, a], dev(2 * c + r, z, y, xc))
        near = pltpu.make_async_copy(src, dst, f_recv.at[xr, a])
        return far, near

    def f_start(a):
        for r in range(2):
            far, near = f_copies(r, a)
            pl.when(x != 2 * c + r)(far.start)
            pl.when(x == 2 * c + r)(near.start)

    gsend[0] = (dqT[...] * SCALE).T.astype(BF)
    f_start(0)

    await_at(aall.at[y * 2 + 1 - c], ya_recv.at[0])
    for k in (1, 2, 3):
        await_at(aall.at[y_slot(k, 1 - c)], yaf_recv.at[k])
    for k in range(1, 8):
        w_wait(k)
    o = jnp.zeros((TOK, TOK), F32)
    for h in range(8):
        o = o + dot(aall[h], w_all[h], NN)
    out_ref[...] = o.astype(BF)

    await_at(sib_in.at[7], sb_recv.at[7])
    for a in range(2):
        value = part[7, a] + sib_in[7, a].astype(F32)
        for direction in range(2):
            await_at(rs_in.at[direction, 0, a], rs_recv.at[direction, 0, a])
            value = value + rs_in[direction, 0, a].astype(F32)
        gsend[a + 1] = value.astype(BF)
        f_start(a + 1)

    for k in range(1, NZ):
        await_at(wg_in.at[(z - k) % NZ], wz_recv.at[k])
    wgt = jnp.zeros((64, TOK), F32)
    for n in range(NZ):
        wgt = wgt + wg_in[n].astype(F32)
    wg_ref[...] = wgt.T.astype(BF)

    for a, ref in enumerate((dq_ref, dk_ref, dv_ref)):
        for e in range(2):
            await_at(gin.at[e, a], f_recv.at[e, a])
            ref[:, e * HD:(e + 1) * HD] = gin[e, a]

    for e in range(2):
        for a in range(3):
            far, _ = a_copies(e, a)
            pl.when(x != 2 * c + e)(far.wait_send)
            far, _ = f_copies(e, a)
            pl.when(x != 2 * c + e)(far.wait_send)
        far, _ = d_copies(e)
        pl.when(x != 2 * c + e)(far.wait_send)
    for k in range(NY):
        y_copies(k, g_ref, g_all, y_send, y_recv).wait_send()
        y_copies(k, own_attn, aall, ya_send, ya_recv).wait_send()
        far, _ = o_copies(k)
        if k:
            y_forward(k, g_all, yf_send, yf_recv).wait_send()
            y_forward(k, aall, yaf_send, yaf_recv).wait_send()
            gx_copy(k).wait_send()
            far.wait_send()
        else:
            pl.when(c != xc)(far.wait_send)
    for k in range(1, 8):
        w_copy(k).wait_send()
        wz_copy(k).wait_send()
    for direction in range(2):
        for dist in range(1, 5):
            for a in range(2):
                if dist < 4 or a == direction:
                    ag_copy(direction, dist, a, z).wait_send()
                    rs_copy(direction, dist, a).wait_send()
    for t in range(8):
        sb_copy(t).wait_send()
        for a in range(2):
            sib_copy(t, a, z).wait_send()


def on_device(queries, key_rows, value_rows, w_out, out_grad, tile_kind):
    vmem = pl.BlockSpec(memory_space=pltpu.VMEM)
    smem = pl.BlockSpec(memory_space=pltpu.SMEM)
    V = pltpu.VMEM
    S = lambda *shape: pltpu.SemaphoreType.DMA(shape)
    D = 2048
    scratch = [
        V((NZ, 2, 2 * HALF, HD), BF),
        V((HALF, HD), BF),
        V((HALF, HD), BF),
        V((NZ, 2, HALF, HALF), BF),
        V((NZ, 2, 1, HALF), F32),
        V((HD, HALF), F32),
        V((HD, HALF), F32),
        V((1, HALF), F32),
        V((1, HALF), F32),
        V((HD, HALF), F32),
        V((HD, HALF), F32),
        V((8, TOK, TOK), BF),
        V((8, TOK, TOK), BF),
        V((TOK, TOK), BF),
        V((NX, 2, TOK, TOK), BF),
        V((HALF, HD), BF),
        V((2, HALF, TOK), BF),
        V((8, TOK, TOK), BF),
        V((8, 2, HALF, HD), F32),
        V((8, 2, HALF, HD), BF),
        V((8, 2, HALF, HD), BF),
        V((2, 4, 2, HALF, HD), BF),
        V((2, 4, 2, HALF, HD), BF),
        V((NZ, 64, TOK), BF),
        V((NZ, 64, TOK), BF),
        V((3, HALF, HD), BF),
        V((2, 3, TOK, HD), BF),
        S(2, 3), S(2, 3), S(2, 4, 2), S(2, 4, 2), S(8, 2), S(8, 2),
        S(4), S(4), S(4), S(4), S(8), S(8), S(2), S(2), S(4), S(4),
        S(4), S(2, 2), S(4), S(4), S(4), S(4),
        S(2, 4, 2), S(2, 4, 2), S(8), S(8), S(8), S(8), S(2, 3), S(2, 3),
    ]
    shape = lambda *s: jax.ShapeDtypeStruct(s, BF)
    return pl.pallas_call(
        kernel,
        out_shape=[shape(TOK, TOK)] * 4 + [shape(TOK, 64)],
        in_specs=[vmem] * 5 + [smem],
        out_specs=[vmem] * 5,
        scratch_shapes=scratch,
        compiler_params=pltpu.CompilerParams(
            collective_id=0, has_side_effects=True, vmem_limit_bytes=56 * 1024 * 1024
        ),
        cost_estimate=pl.CostEstimate(flops=8 * 10**9, bytes_accessed=4 * 10**6, transcendentals=0),
    )(queries, key_rows, value_rows, w_out, out_grad, tile_kind)


def solution(mesh):
    in_specs = (
        P("ctx", "head"),
        P("ctx", "head"),
        P("ctx", "head"),
        P("head", None),
        P("ctx", "head"),
        P(),
    )
    out_specs = (
        P("ctx", "head"),
        P("ctx", "head"),
        P("ctx", "head"),
        P("ctx", "head"),
        P("head", "ctx"),
    )
    return jax.shard_map(
        on_device, mesh=mesh, in_specs=in_specs, out_specs=out_specs, check_vma=False
    )
```

```python
import functools

import jax
import jax.numpy as jnp
from jax import lax
from jax.experimental import pallas as pl
from jax.experimental.pallas import tpu as pltpu
from jax.sharding import PartitionSpec as P

HD = 128
TILE = 128
NX, NY, NZ = 4, 4, 8
TOK = 256
HALF = 512
SCALE = HD ** -0.5
EXP2_SCALE = SCALE * 1.4426950408889634
NEG = -1e30
MESH = pl.DeviceIdType.MESH
BF = jnp.bfloat16
F32 = jnp.float32
NT = (((1,), (1,)), ((), ()))
NN = (((1,), (0,)), ((), ()))
TN = (((0,), (0,)), ((), ()))


def dot(a, b, dims):
    return lax.dot_general(a, b, dims, preferred_element_type=F32)


def kernel(
    q_ref, k_ref, v_ref, w_ref, g_ref, kind_ref,
    out_ref, dq_ref, dk_ref, dv_ref, wg_ref,
    kv, qs, dos, pst, mst, oT, dqT, mrow, lrow, aT, dof,
    w_in, g_all, w_all, dsend, gx, osend, afull, aall,
    part, sib_out, sib_in, rs_out, rs_in, wgp, wz_out, wz_in, gsend, gq, gkv,
    l_sem, a_send, a_recv, ag_send, ag_recv, sib_send, sib_recv,
    y_send, y_recv, yf_send, yf_recv, w_send, w_recv, d_send, d_recv,
    gx_send, gx_recv, gxf_send, gxf_recv,
    o_send, o_recv, ya_send, ya_recv, yaf_send, yaf_recv,
    rs_send, rs_recv, sb_send, sb_recv, wz_send, wz_recv, f_send, f_recv, g_send, g_recv,
):
    i = lax.axis_index("ctx")
    j = lax.axis_index("head")
    x, z = lax.div(i, NZ), lax.rem(i, NZ)
    y, c = lax.div(j, 2), lax.rem(j, 2)
    xc, xr = lax.div(x, 2), lax.rem(x, 2)

    def dev(x_, z_, y_, c_):
        return (x_ * NZ + z_, y_ * 2 + c_)

    def zplus(n):
        return lax.rem(z + (n + NZ), NZ)

    def xplus(n):
        return lax.rem(x + (n + NX), NX)

    def yplus(n):
        return lax.rem(y + (n + NY), NY)

    sibling = dev(x, z, y, 1 - c)

    def remote(src, dst, ss, rs, to):
        return pltpu.make_async_remote_copy(
            src_ref=src, dst_ref=dst, send_sem=ss, recv_sem=rs, device_id=to, device_id_type=MESH
        )

    def await_at(dst, sem):
        pltpu.make_async_copy(dst, dst, sem).wait()

    w_load = pltpu.make_async_copy(w_ref, w_in, l_sem.at[0])
    g_load = pltpu.make_async_copy(g_ref, g_all.at[j], l_sem.at[1])
    g_load.start()
    w_load.start()

    barrier = pltpu.get_barrier_semaphore()
    partners = []
    for dx in range(NX):
        for dc in range(2):
            if dx or dc:
                partners.append(dev(xplus(dx), z, y, c if dc == 0 else 1 - c))
    for dy in range(1, NY):
        for dc in range(2):
            partners.append(dev(x, z, yplus(dy), c if dc == 0 else 1 - c))
    for dz in (1, -1):
        partners.append(dev(x, zplus(dz), y, c))
        for r in range(2):
            partners.append(dev(2 * c + r, zplus(dz), y, xc))
    for to in partners:
        pl.semaphore_signal(barrier, inc=1, device_id=to, device_id_type=MESH)
    pl.semaphore_wait(barrier, len(partners))

    my_rows = pl.ds(pl.multiple_of(x * TOK, TOK), TOK)
    q_rows = pl.ds(pl.multiple_of(xr * TOK, TOK), TOK)
    half_rows = pl.ds(pl.multiple_of(c * HALF, HALF), HALF)

    def start_either(far, near, at):
        pl.when(x != 2 * c + at)(far.start)
        pl.when(x == 2 * c + at)(near.start)

    def a_copies(e, a):
        src = (k_ref, v_ref, q_ref)[a].at[:, pl.ds(e * HD, HD)]
        dst = qs.at[q_rows, :] if a == 2 else kv.at[z, a, my_rows, :]
        far = remote(src, dst, a_send.at[e, a], a_recv.at[xr, a], dev(2 * c + e, z, y, xc))
        near = pltpu.make_async_copy(src, dst, a_recv.at[xr, a])
        return far, near

    for a in range(3):
        for e in range(2):
            start_either(*a_copies(e, a), e)

    def y_copies(k, src, dst, ss, rs):
        if k == 0:
            return remote(src, dst.at[j], ss.at[0], rs.at[0], sibling)
        return remote(src, dst.at[j], ss.at[k], rs.at[k], dev(x, z, yplus(k), c))

    def y_slot(k, core):
        return yplus(-k) * 2 + core

    def y_forward(k, dst, ss, rs):
        slot = y_slot(k, c)
        return remote(dst.at[slot], dst.at[slot], ss.at[k], rs.at[k], sibling)

    for k in (1, 2, 3, 0):
        y_copies(k, g_ref, g_all, y_send, y_recv).start()

    def w_copy(k):
        to = lax.rem(j + k, 8)
        return remote(
            w_in.at[:, pl.ds(pl.multiple_of(to * TOK, TOK), TOK)], w_all.at[j],
            w_send.at[k], w_recv.at[k], (i, to),
        )

    def w_wait(k):
        await_at(w_all.at[lax.rem(j + 8 - k, 8)], w_recv.at[k])

    def ag_copy(direction, dist, a, zs):
        ref = kv.at[zs, a, half_rows, :]
        return remote(
            ref, ref, ag_send.at[direction, dist - 1, a], ag_recv.at[direction, dist - 1, a],
            dev(x, zplus(1 - 2 * direction), y, c),
        )

    def sib_copy(t, a, zs):
        ref = kv.at[zs, a, half_rows, :]
        return remote(ref, ref, sib_send.at[t, a], sib_recv.at[t, a], sibling)

    kpos = lax.broadcasted_iota(jnp.int32, (TILE, HALF), 0)
    qpos = lax.broadcasted_iota(jnp.int32, (TILE, HALF), 1) % TILE
    diff = kpos - qpos

    def block_of(half, b, zs):
        return 2 * ((2 * half + b // 2) * NZ + zs) + b % 2

    def forward_unit(zs, half):
        rows = pl.ds(pl.multiple_of(half * HALF, HALF), HALF)
        s = dot(kv[zs, 0, rows, :], qs[...], NT)
        parts = []
        for kb in range(4):
            limits = []
            for qb in range(4):
                kind = kind_ref[block_of(c, qb, z), block_of(half, kb, zs)]
                limit = jnp.where(kind == 1, 1000, jnp.where(kind == 2, 0, -1000))
                limits.append(jnp.full((1, TILE), limit, jnp.int32))
            limit = jnp.concatenate(limits, axis=1)
            parts.append(jnp.where(diff <= limit, s[kb * TILE:(kb + 1) * TILE, :], NEG))
        s = jnp.concatenate(parts, axis=0)
        old = mrow[...]
        new = jnp.maximum(old, jnp.max(s, axis=0, keepdims=True))
        alpha = jnp.exp2((old - new) * EXP2_SCALE)
        p = jnp.exp2((s - new) * EXP2_SCALE)
        lrow[...] = lrow[...] * alpha + jnp.sum(p, axis=0, keepdims=True)
        mrow[...] = new
        mst[zs, half] = new
        pb = p.astype(BF)
        pst[zs, half] = pb
        oT[...] = oT[...] * alpha + dot(kv[zs, 1, rows, :].T, pb, NN)

    mrow[...] = jnp.full(mrow.shape, NEG, F32)
    lrow[...] = jnp.zeros(lrow.shape, F32)
    oT[...] = jnp.zeros(oT.shape, F32)
    dqT[...] = jnp.zeros(dqT.shape, F32)
    for a in range(2):
        wz_in[a, 3] = jnp.zeros((64, TOK), BF)

    def d_copies(e):
        src = dsend.at[:, pl.ds(e * HD, HD)]
        dst = dos.at[q_rows, :]
        far = remote(src, dst, d_send.at[e], d_recv.at[xr], dev(2 * c + e, z, y, xc))
        near = pltpu.make_async_copy(src, dst, d_recv.at[xr])
        return far, near

    def gx_copy(k):
        to = xplus(k)
        return remote(
            g_all.at[2 * to + c], gx.at[x, c], gx_send.at[k], gx_recv.at[k], dev(to, z, y, c)
        )

    def gx_forward(k):
        ref = gx.at[xplus(-k), c]
        return remote(ref, ref, gxf_send.at[k], gxf_recv.at[k], sibling)

    def forward_step(t, carry):
        dist = lax.div(t + 1, 2)
        odd = lax.rem(t, 2)
        zs = zplus(dist * (1 - 2 * odd))

        @pl.when(t == 0)
        def _():
            for a in range(2):
                for r in range(2):
                    own = pl.ds(pl.multiple_of(c * HALF, HALF) + r * TOK, TOK)
                    await_at(kv.at[z, a, own, :], a_recv.at[r, a])
                for direction in range(2):
                    ag_copy(direction, 1, a, z).start()
                sib_copy(t, a, z).start()
            for r in range(2):
                await_at(qs.at[pl.ds(r * TOK, TOK), :], a_recv.at[r, 2])

        @pl.when((odd == 1) & (t < 7))
        def _():
            for a in range(2):
                for direction in range(2):
                    src = zplus(dist * (2 * direction - 1))
                    await_at(kv.at[src, a, half_rows, :], ag_recv.at[direction, dist - 1, a])
                    forward = ag_copy(direction, dist + 1, a, src)
                    if direction == a:
                        forward.start()
                    else:
                        pl.when(dist < 3)(forward.start)
                    sib_copy(t + direction, a, src).start()

        @pl.when(t == 7)
        def _():
            for a in range(2):
                await_at(kv.at[zs, a, half_rows, :], ag_recv.at[a, 3, a])
                sib_copy(t, a, zs).start()

        @pl.when(t == 1)
        def _():
            for k in (1, 2, 3):
                await_at(g_all.at[y_slot(k, c)], y_recv.at[k])
                y_forward(k, g_all, yf_send, yf_recv).start()
            g_load.wait()
            w_load.wait()

        @pl.when(t == 2)
        def _():
            await_at(g_all.at[y * 2 + 1 - c], y_recv.at[0])
            for k in (1, 2, 3):
                await_at(g_all.at[y_slot(k, 1 - c)], yf_recv.at[k])
            d = jnp.zeros((TOK, TOK), F32)
            for h in range(8):
                d = d + dot(g_all[h], w_in[:, h * TOK:(h + 1) * TOK], NT)
            dsend[...] = d.astype(BF)
            for e in range(2):
                start_either(*d_copies(e), e)
            for k in range(1, NX):
                gx_copy(k).start()
            for k in range(1, 8):
                w_copy(k).start()
            for h in range(2):
                gx[x, h] = g_all[2 * x + h]
            w_all[j] = w_in[:, pl.ds(pl.multiple_of(j * TOK, TOK), TOK)]

        @pl.when(t == 6)
        def _():
            for r in range(2):
                await_at(dos.at[pl.ds(r * TOK, TOK), :], d_recv.at[r])
            dof[...] = dos[...].astype(F32).T

        forward_unit(zs, c)
        for a in range(2):
            other = pl.ds(pl.multiple_of((1 - c) * HALF, HALF), HALF)
            await_at(kv.at[zs, a, other, :], sib_recv.at[t, a])
        forward_unit(zs, 1 - c)
        return carry

    lax.fori_loop(0, 8, forward_step, 0)

    inv = 1.0 / lrow[...]
    attnT = (oT[...] * inv).astype(BF).astype(F32)
    aT[...] = attnT
    osend[...] = attnT.T.astype(BF)

    def o_copies(k):
        dst = afull.at[c, :, pl.ds(pl.multiple_of(xr * HD, HD), HD)]
        far = remote(osend, dst, o_send.at[k], o_recv.at[xr, c], dev(xplus(k), z, y, xc))
        near = pltpu.make_async_copy(osend, dst, o_recv.at[xr, c])
        return far, near

    for k in range(NX):
        far, near = o_copies(k)
        if k:
            far.start()
        else:
            pl.when(c != xc)(far.start)
            pl.when(c == xc)(near.start)

    def sb_copy(u):
        return remote(sib_out.at[u], sib_in.at[u], sb_send.at[u], sb_recv.at[u], sibling)

    def sb_wait(u):
        await_at(sib_in.at[u], sb_recv.at[u])

    def rs_copy(direction, dist, a):
        return remote(
            rs_out.at[direction, dist - 1, a], rs_in.at[direction, dist - 1, a],
            rs_send.at[direction, dist - 1, a], rs_recv.at[direction, dist - 1, a],
            dev(x, zplus(1 - 2 * direction), y, c),
        )

    def g_copy(direction, r, a):
        return remote(
            rs_out.at[direction, 0, a, pl.ds(r * TOK, TOK), :], gkv.at[direction, xr, a],
            g_send.at[direction, r, a], g_recv.at[direction, xr, a],
            dev(2 * c + r, zplus(1 - 2 * direction), y, xc),
        )

    def total(u, a):
        return part[u, a] + sib_in[u, a].astype(F32)

    def ring(direction, dist, a):
        value = total(0 if dist == 4 else 7 - 2 * dist + direction, a)
        if dist < 3 or (dist == 3 and a == direction):
            await_at(rs_in.at[direction, dist, a], rs_recv.at[direction, dist, a])
            value = value + rs_in[direction, dist, a].astype(F32)
        rs_out[direction, dist - 1, a] = value.astype(BF)
        if dist > 1:
            rs_copy(direction, dist, a).start()
        else:
            for r in range(2):
                g_copy(direction, r, a).start()

    def wz_copy(direction, dist):
        src, dst = wz_out.at[direction, dist - 1], wz_in.at[direction, dist - 1]
        if dist == 4:
            rows = pl.ds(32 * direction, 32)
            src, dst = src.at[rows, :], dst.at[rows, :]
        return remote(
            src, dst, wz_send.at[direction, dist - 1], wz_recv.at[direction, dist - 1],
            dev(x, zplus(1 - 2 * direction), y, c),
        )

    def wz_wait(direction, dist):
        dst = wz_in.at[direction, dist]
        if dist == 3:
            dst = dst.at[pl.ds(32 * direction, 32), :]
        await_at(dst, wz_recv.at[direction, dist])

    def wz_step(dist):
        for direction in range(2):
            value = wgp[zplus(dist * (1 - 2 * direction))]
            if dist < 4:
                wz_wait(direction, dist)
                value = value + wz_in[direction, dist].astype(F32)
            wz_out[direction, dist - 1] = value.astype(BF)
            wz_copy(direction, dist).start()

    def backward_unit(zs, half):
        rows = pl.ds(pl.multiple_of(half * HALF, HALF), HALF)
        factor = jnp.exp2((mst[zs, half] - mrow[...]) * EXP2_SCALE) / lrow[...]
        dob = (dof[...] * factor).astype(BF)
        delta = jnp.sum(dob.astype(F32) * aT[...], axis=0, keepdims=True)
        p = pst[zs, half]
        dv = dot(p, dob, NT)
        dp = dot(kv[zs, 1, rows, :], dob, NN)
        ds = (p.astype(F32) * (dp - delta)).astype(BF)
        dk = dot(ds, qs[...], NN) * SCALE
        dqT[...] += dot(kv[zs, 0, rows, :].T, ds, NN)
        return dk, dv

    own_attn = afull.at[xc, q_rows, :]

    def backward_step(u, carry):
        dist = lax.div(8 - u, 2)
        odd = lax.rem(u, 2)
        zs = zplus(dist * (2 * odd - 1))
        dk, dv = backward_unit(zs, 1 - c)
        sib_out[u, 0] = dk.astype(BF)
        sib_out[u, 1] = dv.astype(BF)
        sb_copy(u).start()
        dk, dv = backward_unit(zs, c)
        part[u, 0] = dk
        part[u, 1] = dv

        @pl.when(u == 0)
        def _():
            sb_wait(0)
            for a in range(2):
                ring(a, 4, a)

        @pl.when(u == 1)
        def _():
            for k in range(1, NX):
                await_at(gx.at[xplus(-k), c], gx_recv.at[k])
                gx_forward(k).start()

        @pl.when(u == 2)
        def _():
            sb_wait(1)
            sb_wait(2)
            for direction in range(2):
                ring(direction, 3, 1 - direction)

        @pl.when(u == 4)
        def _():
            for direction in range(2):
                ring(direction, 3, direction)

        @pl.when(u == 6)
        def _():
            sb_wait(3)
            sb_wait(4)
            for direction in range(2):
                ring(direction, 2, 1 - direction)
            for e in range(2):
                for half in range(2):
                    await_at(afull.at[half, :, pl.ds(e * HD, HD)], o_recv.at[e, half])
            for k in (1, 2, 3, 0):
                y_copies(k, own_attn, aall, ya_send, ya_recv).start()
            for k in range(1, NX):
                await_at(gx.at[xplus(-k), 1 - c], gxf_recv.at[k])
            for h in range(2):
                wg = jnp.zeros((TOK, TOK), F32)
                for xx in range(NX):
                    at = afull[xx // 2, (xx % 2) * TOK:(xx % 2 + 1) * TOK, :]
                    wg = wg + dot(gx[xx, h], at, TN)
                for n in range(4):
                    wgp[4 * h + n] = wg[n * 64:(n + 1) * 64, :]
            wz_step(4)
            aall[j] = own_attn[...]

        return carry

    lax.fori_loop(0, 8, backward_step, 0)

    for direction in range(2):
        ring(direction, 2, direction)

    def f_copies(r, a):
        src = gsend.at[a, pl.ds(r * TOK, TOK), :]
        dst = gkv.at[2, xr, a] if a < 2 else gq.at[xr]
        far = remote(src, dst, f_send.at[r, a], f_recv.at[xr, a], dev(2 * c + r, z, y, xc))
        near = pltpu.make_async_copy(src, dst, f_recv.at[xr, a])
        return far, near

    gsend[2] = (dqT[...] * SCALE).T.astype(BF)
    sb_wait(7)
    for a in range(2):
        gsend[a] = total(7, a).astype(BF)
    for a in range(3):
        for r in range(2):
            start_either(*f_copies(r, a), r)
    wz_step(3)
    sb_wait(5)
    sb_wait(6)
    for direction in range(2):
        ring(direction, 1, 1 - direction)
    wz_step(2)
    for direction in range(2):
        ring(direction, 1, direction)
    for k in (1, 2, 3):
        await_at(aall.at[y_slot(k, c)], ya_recv.at[k])
        y_forward(k, aall, yaf_send, yaf_recv).start()
    wz_step(1)

    for k in range(1, 8):
        w_wait(k)
    await_at(aall.at[y * 2 + 1 - c], ya_recv.at[0])
    for k in (1, 2, 3):
        await_at(aall.at[y_slot(k, 1 - c)], yaf_recv.at[k])
    o = jnp.zeros((TOK, TOK), F32)
    for h in range(8):
        o = o + dot(aall[h], w_all[h], NN)
    out_ref[...] = o.astype(BF)

    for e in range(2):
        for a in range(3):
            far, _ = a_copies(e, a)
            pl.when(x != 2 * c + e)(far.wait_send)
            far, _ = f_copies(e, a)
            pl.when(x != 2 * c + e)(far.wait_send)
        far, _ = d_copies(e)
        pl.when(x != 2 * c + e)(far.wait_send)
    for k in range(NY):
        y_copies(k, g_ref, g_all, y_send, y_recv).wait_send()
        y_copies(k, own_attn, aall, ya_send, ya_recv).wait_send()
        far, _ = o_copies(k)
        if k:
            y_forward(k, g_all, yf_send, yf_recv).wait_send()
            y_forward(k, aall, yaf_send, yaf_recv).wait_send()
            gx_copy(k).wait_send()
            gx_forward(k).wait_send()
            far.wait_send()
        else:
            pl.when(c != xc)(far.wait_send)
    for k in range(1, 8):
        w_copy(k).wait_send()
    for t in range(8):
        sb_copy(t).wait_send()
        for a in range(2):
            sib_copy(t, a, z).wait_send()
    for direction in range(2):
        for dist in range(1, 5):
            for a in range(2):
                if dist < 4 or a == direction:
                    ag_copy(direction, dist, a, z).wait_send()
                    if dist > 1:
                        rs_copy(direction, dist, a).wait_send()

    for e in range(2):
        await_at(gq.at[e], f_recv.at[e, 2])
        dq_ref[:, e * HD:(e + 1) * HD] = gq[e]
    for e in range(2):
        for a in range(2):
            await_at(gkv.at[2, e, a], f_recv.at[e, a])

    for direction in range(2):
        wz_wait(direction, 0)
    wg_ref[...] = (wgp[z] + wz_in[0, 0].astype(F32) + wz_in[1, 0].astype(F32)).astype(BF)
    for direction in range(2):
        for dist in range(1, 5):
            wz_copy(direction, dist).wait_send()

    for a, ref in ((1, dv_ref), (0, dk_ref)):
        for e in range(2):
            for direction in range(2):
                await_at(gkv.at[direction, e, a], g_recv.at[direction, e, a])
            value = gkv[0, e, a].astype(F32) + gkv[1, e, a].astype(F32) + gkv[2, e, a].astype(F32)
            ref[:, e * HD:(e + 1) * HD] = value.astype(BF)
    for direction in range(2):
        for r in range(2):
            for a in range(2):
                g_copy(direction, r, a).wait_send()


def copy_kernel(*refs):
    for n in range(5):
        refs[5 + n][...] = refs[n][...]


def on_device(queries, key_rows, value_rows, w_out, out_grad, tile_kind):
    vmem = pl.BlockSpec(memory_space=pltpu.VMEM)
    smem = pl.BlockSpec(memory_space=pltpu.SMEM)
    anywhere = pl.BlockSpec(memory_space=pl.ANY)
    V = pltpu.VMEM
    S = lambda *shape: pltpu.SemaphoreType.DMA(shape)
    scratch = [
        V((NZ, 2, 2 * HALF, HD), BF),
        V((HALF, HD), BF),
        V((HALF, HD), BF),
        V((NZ, 2, HALF, HALF), BF),
        V((NZ, 2, 1, HALF), F32),
        V((HD, HALF), F32),
        V((HD, HALF), F32),
        V((1, HALF), F32),
        V((1, HALF), F32),
        V((HD, HALF), F32),
        V((HD, HALF), F32),
        V((TOK, 8 * TOK), BF),
        V((8, TOK, TOK), BF),
        V((8, TOK, TOK), BF),
        V((TOK, TOK), BF),
        V((NX, 2, TOK, TOK), BF),
        V((HALF, HD), BF),
        V((2, HALF, TOK), BF),
        V((8, TOK, TOK), BF),
        V((8, 2, HALF, HD), F32),
        V((8, 2, HALF, HD), BF),
        V((8, 2, HALF, HD), BF),
        V((2, 4, 2, HALF, HD), BF),
        V((2, 4, 2, HALF, HD), BF),
        V((NZ, 64, TOK), F32),
        V((2, 4, 64, TOK), BF),
        V((2, 4, 64, TOK), BF),
        V((3, HALF, HD), BF),
        V((2, TOK, HD), BF),
        V((3, 2, 2, TOK, HD), BF),
        S(2), S(2, 3), S(2, 3), S(2, 4, 2), S(2, 4, 2), S(8, 2), S(8, 2),
        S(4), S(4), S(4), S(4), S(8), S(8), S(2), S(2),
        S(4), S(4), S(4), S(4),
        S(4), S(2, 2), S(4), S(4), S(4), S(4),
        S(2, 4, 2), S(2, 4, 2), S(8), S(8), S(2, 4), S(2, 4), S(2, 3), S(2, 3),
        S(2, 2, 2), S(2, 2, 2),
    ]
    shape = lambda *s: jax.ShapeDtypeStruct(s, BF)
    outs = [shape(TOK, TOK)] * 4 + [shape(64, TOK)]
    held = pl.pallas_call(
        kernel,
        out_shape=outs,
        in_specs=[anywhere] * 5 + [smem],
        out_specs=[vmem] * 5,
        scratch_shapes=scratch,
        compiler_params=pltpu.CompilerParams(
            collective_id=0, has_side_effects=True, vmem_limit_bytes=56 * 1024 * 1024
        ),
        cost_estimate=pl.CostEstimate(flops=8 * 10**9, bytes_accessed=4 * 10**6, transcendentals=0),
    )(queries, key_rows, value_rows, w_out, out_grad, tile_kind)
    out, dq, dk, dv, wg = pl.pallas_call(
        copy_kernel, out_shape=outs, in_specs=[vmem] * 5, out_specs=[vmem] * 5
    )(*held)
    return out, dq, dk, dv, wg.T


def solution(mesh):
    in_specs = (
        P("ctx", "head"),
        P("ctx", "head"),
        P("ctx", "head"),
        P("head", None),
        P("ctx", "head"),
        P(),
    )
    out_specs = (
        P("ctx", "head"),
        P("ctx", "head"),
        P("ctx", "head"),
        P("ctx", "head"),
        P("head", "ctx"),
    )
    return jax.shard_map(
        on_device, mesh=mesh, in_specs=in_specs, out_specs=out_specs, check_vma=False
    )
```

```python
import functools

import jax
import jax.numpy as jnp
from jax import lax
from jax.experimental import pallas as pl
from jax.experimental.pallas import tpu as pltpu
from jax.sharding import PartitionSpec as P

HD = 128
TILE = 128
NX, NY, NZ = 4, 4, 8
TOK = 256
HALF = 512
SCALE = HD ** -0.5
EXP2_SCALE = SCALE * 1.4426950408889634
NEG = -1e30
MESH = pl.DeviceIdType.MESH
BF = jnp.bfloat16
F32 = jnp.float32
NT = (((1,), (1,)), ((), ()))
NN = (((1,), (0,)), ((), ()))
TN = (((0,), (0,)), ((), ()))


def dot(a, b, dims):
    return lax.dot_general(a, b, dims, preferred_element_type=F32)


def kernel(
    q_ref, k_ref, v_ref, w_ref, g_ref, kind_ref,
    out_ref, dq_ref, dk_ref, dv_ref, wg_ref,
    kv, qs, dos, pst, mst, oT, dqT, mrow, lrow, aT, dof,
    w_in, g_all, w_all, dsend, gx, osend, afull, aall,
    part, sib_out, sib_in, rs_out, rs_in, wgp, wz_out, wz_in, gsend, gq, gkv,
    l_sem, a_send, a_recv, ag_send, ag_recv, sib_send, sib_recv,
    y_send, y_recv, yf_send, yf_recv, w_send, w_recv, d_send, d_recv,
    gx_send, gx_recv, gxf_send, gxf_recv,
    o_send, o_recv, ya_send, ya_recv, yaf_send, yaf_recv,
    rs_send, rs_recv, sb_send, sb_recv, wz_send, wz_recv, f_send, f_recv, g_send, g_recv,
):
    i = lax.axis_index("ctx")
    j = lax.axis_index("head")
    x, z = lax.div(i, NZ), lax.rem(i, NZ)
    y, c = lax.div(j, 2), lax.rem(j, 2)
    xc, xr = lax.div(x, 2), lax.rem(x, 2)

    def dev(x_, z_, y_, c_):
        return (x_ * NZ + z_, y_ * 2 + c_)

    def zplus(n):
        return lax.rem(z + (n + NZ), NZ)

    def xplus(n):
        return lax.rem(x + (n + NX), NX)

    def yplus(n):
        return lax.rem(y + (n + NY), NY)

    sibling = dev(x, z, y, 1 - c)

    def remote(src, dst, ss, rs, to):
        return pltpu.make_async_remote_copy(
            src_ref=src, dst_ref=dst, send_sem=ss, recv_sem=rs, device_id=to, device_id_type=MESH
        )

    def await_at(dst, sem):
        pltpu.make_async_copy(dst, dst, sem).wait()

    w_load = pltpu.make_async_copy(w_ref, w_in, l_sem.at[0])
    g_load = pltpu.make_async_copy(g_ref, g_all.at[j], l_sem.at[1])
    g_load.start()
    w_load.start()

    barrier = pltpu.get_barrier_semaphore()
    partners = []
    for dz in (2, -2):
        partners.append(dev(x, zplus(dz), y, c))
    for dx in (2, 1, 3):
        for core in (c, 1 - c):
            partners.append(dev(xplus(dx), z, y, core))
    for dy in (2, 1, 3):
        for core in (c, 1 - c):
            partners.append(dev(x, z, yplus(dy), core))
    for dz in (1, -1):
        for r in range(2):
            partners.append(dev(2 * c + r, zplus(dz), y, xc))
        partners.append(dev(x, zplus(dz), y, c))
    partners.append(sibling)
    for to in partners:
        pl.semaphore_signal(barrier, inc=1, device_id=to, device_id_type=MESH)
    pl.semaphore_wait(barrier, len(partners))

    my_rows = pl.ds(pl.multiple_of(x * TOK, TOK), TOK)
    q_rows = pl.ds(pl.multiple_of(xr * TOK, TOK), TOK)
    half_rows = pl.ds(pl.multiple_of(c * HALF, HALF), HALF)

    def start_either(far, near, at):
        pl.when(x != 2 * c + at)(far.start)
        pl.when(x == 2 * c + at)(near.start)

    def a_copies(e, a):
        src = (k_ref, v_ref, q_ref)[a].at[:, pl.ds(e * HD, HD)]
        dst = qs.at[q_rows, :] if a == 2 else kv.at[z, a, my_rows, :]
        far = remote(src, dst, a_send.at[e, a], a_recv.at[xr, a], dev(2 * c + e, z, y, xc))
        near = pltpu.make_async_copy(src, dst, a_recv.at[xr, a])
        return far, near

    for a in range(3):
        for e in range(2):
            start_either(*a_copies(e, a), e)

    def y_copies(k, src, dst, ss, rs):
        if k == 0:
            return remote(src, dst.at[j], ss.at[0], rs.at[0], sibling)
        return remote(src, dst.at[j], ss.at[0], rs.at[k], dev(x, z, yplus(k), c))

    def y_slot(k, core):
        return yplus(-k) * 2 + core

    def y_forward(k, dst, ss, rs):
        slot = y_slot(k, c)
        return remote(dst.at[slot], dst.at[slot], ss.at[0], rs.at[k], sibling)

    for k in (1, 2, 3, 0):
        y_copies(k, g_ref, g_all, y_send, y_recv).start()

    def w_copy(k):
        to = lax.rem(j + k, 8)
        return remote(
            w_in.at[:, pl.ds(pl.multiple_of(to * TOK, TOK), TOK)], w_all.at[j],
            w_send.at[0], w_recv.at[k], (i, to),
        )

    def w_wait(k):
        await_at(w_all.at[lax.rem(j + 8 - k, 8)], w_recv.at[k])

    def piece(zs, a, r):
        return kv.at[zs, a, pl.ds(pl.multiple_of(c * HALF + r * TOK, TOK), TOK), :]

    def ag_copy(direction, dist, a, r, zs):
        ref = piece(zs, a, r)
        return remote(
            ref, ref, ag_send.at[direction, dist - 1], ag_recv.at[direction, dist - 1, a, r],
            dev(x, zplus(1 - 2 * direction), y, c),
        )

    def sib_copy(t, a, zs):
        ref = kv.at[zs, a, half_rows, :]
        return remote(ref, ref, sib_send.at[0], sib_recv.at[t, a], sibling)

    kpos = lax.broadcasted_iota(jnp.int32, (TILE, HALF), 0)
    qpos = lax.broadcasted_iota(jnp.int32, (TILE, HALF), 1) % TILE
    diff = kpos - qpos

    def block_of(half, b, zs):
        return 2 * ((2 * half + b // 2) * NZ + zs) + b % 2

    def forward_unit(zs, half):
        rows = pl.ds(pl.multiple_of(half * HALF, HALF), HALF)
        s = dot(kv[zs, 0, rows, :], qs[...], NT)
        parts = []
        for kb in range(4):
            limits = []
            for qb in range(4):
                kind = kind_ref[block_of(c, qb, z), block_of(half, kb, zs)]
                limit = jnp.where(kind == 1, 1000, jnp.where(kind == 2, 0, -1000))
                limits.append(jnp.full((1, TILE), limit, jnp.int32))
            limit = jnp.concatenate(limits, axis=1)
            parts.append(jnp.where(diff <= limit, s[kb * TILE:(kb + 1) * TILE, :], NEG))
        s = jnp.concatenate(parts, axis=0)
        old = mrow[...]
        new = jnp.maximum(old, jnp.max(s, axis=0, keepdims=True))
        alpha = jnp.exp2((old - new) * EXP2_SCALE)
        p = jnp.exp2((s - new) * EXP2_SCALE)
        lrow[...] = lrow[...] * alpha + jnp.sum(p, axis=0, keepdims=True)
        mrow[...] = new
        mst[zs, half] = new
        pb = p.astype(BF)
        pst[zs, half] = pb
        oT[...] = oT[...] * alpha + dot(kv[zs, 1, rows, :].T, pb, NN)

    mrow[...] = jnp.full(mrow.shape, NEG, F32)
    lrow[...] = jnp.zeros(lrow.shape, F32)
    oT[...] = jnp.zeros(oT.shape, F32)
    dqT[...] = jnp.zeros(dqT.shape, F32)
    for a in range(2):
        wz_in[1, a] = jnp.zeros((64, TOK), BF)

    def d_copies(e):
        src = dsend.at[:, pl.ds(e * HD, HD)]
        dst = dos.at[q_rows, :]
        far = remote(src, dst, d_send.at[e], d_recv.at[xr], dev(2 * c + e, z, y, xc))
        near = pltpu.make_async_copy(src, dst, d_recv.at[xr])
        return far, near

    def gx_copy(k):
        to = xplus(k)
        return remote(
            g_all.at[2 * to + c], gx.at[x, c], gx_send.at[0], gx_recv.at[k], dev(to, z, y, c)
        )

    def gx_forward(k):
        ref = gx.at[xplus(-k), c]
        return remote(ref, ref, gxf_send.at[0], gxf_recv.at[k], sibling)

    def forward_step(t, carry):
        dist = lax.div(t + 1, 2)
        odd = lax.rem(t, 2)
        zs = zplus(dist * (1 - 2 * odd))

        def arrival(a, r, dist):
            for direction in range(2):
                src = zplus(dist * (2 * direction - 1))
                await_at(piece(src, a, r), ag_recv.at[direction, dist - 1, a, r])
                pl.when((dist < 3) | (a == direction))(
                    ag_copy(direction, dist + 1, a, r, src).start
                )
                pl.when(r == 1)(sib_copy(2 * dist - 1 + direction, a, src).start)

        def slot(s):
            e = s + 1

            @pl.when((s > 2) & (s < 11))
            def _():
                arrival(lax.rem(lax.div(e, 2), 2), lax.rem(e, 2), lax.div(e, 4) + 1)

        @pl.when(t == 0)
        def _():
            for a in range(2):
                for r in range(2):
                    await_at(piece(z, a, r), a_recv.at[r, a])
                    for direction in range(2):
                        ag_copy(direction, 1, a, r, z).start()
                sib_copy(t, a, z).start()
            for r in range(2):
                await_at(qs.at[pl.ds(r * TOK, TOK), :], a_recv.at[r, 2])

        @pl.when(t == 1)
        def _():
            for a in range(2):
                for r in range(2):
                    arrival(jnp.int32(a), jnp.int32(r), jnp.int32(1))

        @pl.when(t == 7)
        def _():
            for r in range(2):
                for a in range(2):
                    await_at(piece(zs, a, r), ag_recv.at[a, 3, a, r])
            for a in range(2):
                sib_copy(t, a, zs).start()

        slot(2 * t)

        @pl.when(t == 1)
        def _():
            for k in (1, 2, 3):
                await_at(g_all.at[y_slot(k, c)], y_recv.at[k])
                y_forward(k, g_all, yf_send, yf_recv).start()
            g_load.wait()
            w_load.wait()

        @pl.when(t == 2)
        def _():
            await_at(g_all.at[y * 2 + 1 - c], y_recv.at[0])
            for k in (1, 2, 3):
                await_at(g_all.at[y_slot(k, 1 - c)], yf_recv.at[k])
            d = jnp.zeros((TOK, TOK), F32)
            for h in range(8):
                d = d + dot(g_all[h], w_in[:, h * TOK:(h + 1) * TOK], NT)
            dsend[...] = d.astype(BF)
            for e in range(2):
                start_either(*d_copies(e), e)
            for k in range(1, NX):
                gx_copy(k).start()

        @pl.when(t == 3)
        def _():
            for k in range(1, 8):
                w_copy(k).start()
            for h in range(2):
                gx[x, h] = g_all[2 * x + h]
            w_all[j] = w_in[:, pl.ds(pl.multiple_of(j * TOK, TOK), TOK)]

        @pl.when(t == 6)
        def _():
            for r in range(2):
                await_at(dos.at[pl.ds(r * TOK, TOK), :], d_recv.at[r])
            dof[...] = dos[...].astype(F32).T

        forward_unit(zs, c)
        slot(2 * t + 1)
        for a in range(2):
            other = pl.ds(pl.multiple_of((1 - c) * HALF, HALF), HALF)
            await_at(kv.at[zs, a, other, :], sib_recv.at[t, a])
        forward_unit(zs, 1 - c)
        return carry

    lax.fori_loop(0, 8, forward_step, 0)

    inv = 1.0 / lrow[...]
    attnT = (oT[...] * inv).astype(BF).astype(F32)
    aT[...] = attnT
    osend[...] = attnT.T.astype(BF)

    def o_copies(k):
        dst = afull.at[c, :, pl.ds(pl.multiple_of(xr * HD, HD), HD)]
        far = remote(osend, dst, o_send.at[k], o_recv.at[xr, c], dev(xplus(k), z, y, xc))
        near = pltpu.make_async_copy(osend, dst, o_recv.at[xr, c])
        return far, near

    for k in range(NX):
        far, near = o_copies(k)
        if k:
            far.start()
        else:
            pl.when(c != xc)(far.start)
            pl.when(c == xc)(near.start)

    def sb_copy(u):
        return remote(sib_out.at[u], sib_in.at[u], sb_send.at[0], sb_recv.at[u], sibling)

    def sb_wait(u):
        await_at(sib_in.at[u], sb_recv.at[u])

    def rs_copy(direction, dist, a):
        return remote(
            rs_out.at[direction, dist - 1, a], rs_in.at[direction, dist - 1, a],
            rs_send.at[0 if dist == 4 else 1], rs_recv.at[direction, dist - 1, a],
            dev(x, zplus(1 - 2 * direction), y, c),
        )

    def g_copy(direction, r, a):
        return remote(
            rs_out.at[direction, 0, a, pl.ds(r * TOK, TOK), :], gkv.at[direction, xr, a],
            g_send.at[direction, r, a], g_recv.at[direction, xr, a],
            dev(2 * c + r, zplus(1 - 2 * direction), y, xc),
        )

    def total(u, a):
        return part[u, a] + sib_in[u, a].astype(F32)

    def ring(direction, dist, a):
        value = total(0 if dist == 4 else 7 - 2 * dist + direction, a)
        if dist < 3 or (dist == 3 and a == direction):
            await_at(rs_in.at[direction, dist, a], rs_recv.at[direction, dist, a])
            value = value + rs_in[direction, dist, a].astype(F32)
        rs_out[direction, dist - 1, a] = value.astype(BF)
        if dist > 1:
            rs_copy(direction, dist, a).start()
        else:
            for r in range(2):
                g_copy(direction, r, a).start()

    def wz_copy(kind, direction):
        src, dst = wz_out.at[kind, direction], wz_in.at[kind, direction]
        if kind == 1:
            rows = pl.ds(32 * direction, 32)
            src, dst = src.at[rows, :], dst.at[rows, :]
        far = (1, 2, 1, 2)[kind] * (1 - 2 * direction)
        return remote(
            src, dst, wz_send.at[0 if kind == 1 else 1], wz_recv.at[kind, direction],
            dev(x, zplus(far), y, c),
        )

    def wz_wait(kind, direction):
        dst = wz_in.at[kind, direction]
        if kind == 1:
            dst = dst.at[pl.ds(32 * direction, 32), :]
        await_at(dst, wz_recv.at[kind, direction])

    def wz_start():
        for kind in (1, 0, 2):
            for direction in range(2):
                to = zplus((3, 4, 1)[kind] * (1 - 2 * direction))
                wz_out[kind, direction] = wgp[to].astype(BF)
                wz_copy(kind, direction).start()

    def wz_middle():
        for direction in range(2):
            for kind in (1, 0):
                wz_wait(kind, direction)
            value = wgp[zplus(2 - 4 * direction)]
            value = value + wz_in[0, direction].astype(F32) + wz_in[1, direction].astype(F32)
            wz_out[3, direction] = value.astype(BF)
            wz_copy(3, direction).start()

    def backward_unit(zs, half):
        rows = pl.ds(pl.multiple_of(half * HALF, HALF), HALF)
        factor = jnp.exp2((mst[zs, half] - mrow[...]) * EXP2_SCALE) / lrow[...]
        dob = (dof[...] * factor).astype(BF)
        delta = jnp.sum(dob.astype(F32) * aT[...], axis=0, keepdims=True)
        p = pst[zs, half]
        dv = dot(p, dob, NT)
        dp = dot(kv[zs, 1, rows, :], dob, NN)
        ds = (p.astype(F32) * (dp - delta)).astype(BF)
        dk = dot(ds, qs[...], NN) * SCALE
        dqT[...] += dot(kv[zs, 0, rows, :].T, ds, NN)
        return dk, dv

    own_attn = afull.at[xc, q_rows, :]

    def f_copies(r, a):
        src = gsend.at[a, pl.ds(r * TOK, TOK), :]
        dst = gkv.at[2, xr, a] if a < 2 else gq.at[xr]
        far = remote(src, dst, f_send.at[r, a], f_recv.at[xr, a], dev(2 * c + r, z, y, xc))
        near = pltpu.make_async_copy(src, dst, f_recv.at[xr, a])
        return far, near

    def backward_step(n, carry):
        u = jnp.where(n == 5, 7, jnp.where(n > 5, n - 1, n))
        dist = lax.div(8 - u, 2)
        odd = lax.rem(u, 2)
        zs = zplus(dist * (2 * odd - 1))
        dk, dv = backward_unit(zs, 1 - c)
        sib_out[u, 0] = dk.astype(BF)
        sib_out[u, 1] = dv.astype(BF)
        sb_copy(u).start()
        dk, dv = backward_unit(zs, c)
        part[u, 0] = dk
        part[u, 1] = dv

        @pl.when(u == 0)
        def _():
            sb_wait(0)
            for a in range(2):
                ring(a, 4, a)

        @pl.when(u == 1)
        def _():
            for k in range(1, NX):
                await_at(gx.at[xplus(-k), c], gx_recv.at[k])
                gx_forward(k).start()

        @pl.when(u == 2)
        def _():
            sb_wait(1)
            sb_wait(2)
            for direction in range(2):
                ring(direction, 3, 1 - direction)

        @pl.when(u == 3)
        def _():
            for direction in range(2):
                ring(direction, 3, direction)

        @pl.when(u == 7)
        def _():
            sb_wait(3)
            sb_wait(4)
            for direction in range(2):
                ring(direction, 2, 1 - direction)
            sb_wait(7)
            for a in range(2):
                gsend[a] = total(7, a).astype(BF)
                for r in range(2):
                    start_either(*f_copies(r, a), r)
            for e in range(2):
                for half in range(2):
                    await_at(afull.at[half, :, pl.ds(e * HD, HD)], o_recv.at[e, half])
            for k in (1, 2, 3, 0):
                y_copies(k, own_attn, aall, ya_send, ya_recv).start()
            for k in range(1, NX):
                await_at(gx.at[xplus(-k), 1 - c], gxf_recv.at[k])
            for h in range(2):
                wg = jnp.zeros((TOK, TOK), F32)
                for xx in range(NX):
                    at = afull[xx // 2, (xx % 2) * TOK:(xx % 2 + 1) * TOK, :]
                    wg = wg + dot(gx[xx, h], at, TN)
                for n in range(4):
                    wgp[4 * h + n] = wg[n * 64:(n + 1) * 64, :]
            wz_start()
            aall[j] = own_attn[...]

        @pl.when(u == 5)
        def _():
            for direction in range(2):
                ring(direction, 2, direction)

        return carry

    lax.fori_loop(0, 8, backward_step, 0)

    gsend[2] = (dqT[...] * SCALE).T.astype(BF)
    for r in range(2):
        start_either(*f_copies(r, 2), r)
    sb_wait(5)
    sb_wait(6)
    for direction in range(2):
        ring(direction, 1, 1 - direction)
    wz_middle()
    for direction in range(2):
        ring(direction, 1, direction)
    for k in (1, 2, 3):
        await_at(aall.at[y_slot(k, c)], ya_recv.at[k])
        y_forward(k, aall, yaf_send, yaf_recv).start()

    for k in range(1, 8):
        w_wait(k)
    await_at(aall.at[y * 2 + 1 - c], ya_recv.at[0])
    for k in (1, 2, 3):
        await_at(aall.at[y_slot(k, 1 - c)], yaf_recv.at[k])
    o = jnp.zeros((TOK, TOK), F32)
    for h in range(8):
        o = o + dot(aall[h], w_all[h], NN)
    out_ref[...] = o.astype(BF)

    for e in range(2):
        for a in range(3):
            far, _ = a_copies(e, a)
            pl.when(x != 2 * c + e)(far.wait_send)
            far, _ = f_copies(e, a)
            pl.when(x != 2 * c + e)(far.wait_send)
        far, _ = d_copies(e)
        pl.when(x != 2 * c + e)(far.wait_send)
    far, _ = o_copies(0)
    pl.when(c != xc)(far.wait_send)
    for k in range(1, NX):
        far, _ = o_copies(k)
        far.wait_send()

    def left(ref, sem):
        remote(ref, ref, sem, sem, sibling).wait_send()

    left(g_all.at[pl.ds(0, 4)], y_send.at[0])
    left(g_all.at[pl.ds(0, 4)], ya_send.at[0])
    for sem in (yf_send, yaf_send, gx_send, gxf_send):
        left(g_all.at[pl.ds(0, 3)], sem.at[0])
    left(w_all.at[pl.ds(0, 7)], w_send.at[0])
    left(sib_out, sb_send.at[0])
    left(kv.at[:, :, pl.ds(0, HALF), :], sib_send.at[0])
    left(rs_out.at[0, 3], rs_send.at[0])
    left(rs_out.at[:, pl.ds(1, 2)], rs_send.at[1])
    for direction in range(2):
        for dist in range(1, 4):
            left(kv.at[0, :, pl.ds(0, HALF), :], ag_send.at[direction, dist - 1])
        left(kv.at[0, 0, pl.ds(0, HALF), :], ag_send.at[direction, 3])

    for e in range(2):
        await_at(gq.at[e], f_recv.at[e, 2])
        dq_ref[:, e * HD:(e + 1) * HD] = gq[e]
    for e in range(2):
        for a in range(2):
            await_at(gkv.at[2, e, a], f_recv.at[e, a])

    wg = wgp[z]
    for kind in (2, 3):
        for direction in range(2):
            wz_wait(kind, direction)
            wg = wg + wz_in[kind, direction].astype(F32)
    wg_ref[...] = wg.astype(BF)
    left(wz_out.at[0, 0], wz_send.at[0])
    left(wz_out.at[pl.ds(0, 3)], wz_send.at[1])

    for a, ref in ((1, dv_ref), (0, dk_ref)):
        for e in range(2):
            for direction in range(2):
                await_at(gkv.at[direction, e, a], g_recv.at[direction, e, a])
            value = gkv[0, e, a].astype(F32) + gkv[1, e, a].astype(F32) + gkv[2, e, a].astype(F32)
            ref[:, e * HD:(e + 1) * HD] = value.astype(BF)
    for direction in range(2):
        for r in range(2):
            for a in range(2):
                g_copy(direction, r, a).wait_send()


def copy_kernel(*refs):
    for n in range(5):
        refs[5 + n][...] = refs[n][...]


def on_device(queries, key_rows, value_rows, w_out, out_grad, tile_kind):
    vmem = pl.BlockSpec(memory_space=pltpu.VMEM)
    smem = pl.BlockSpec(memory_space=pltpu.SMEM)
    anywhere = pl.BlockSpec(memory_space=pl.ANY)
    V = pltpu.VMEM
    S = lambda *shape: pltpu.SemaphoreType.DMA(shape)
    scratch = [
        V((NZ, 2, 2 * HALF, HD), BF),
        V((HALF, HD), BF),
        V((HALF, HD), BF),
        V((NZ, 2, HALF, HALF), BF),
        V((NZ, 2, 1, HALF), F32),
        V((HD, HALF), F32),
        V((HD, HALF), F32),
        V((1, HALF), F32),
        V((1, HALF), F32),
        V((HD, HALF), F32),
        V((HD, HALF), F32),
        V((TOK, 8 * TOK), BF),
        V((8, TOK, TOK), BF),
        V((8, TOK, TOK), BF),
        V((TOK, TOK), BF),
        V((NX, 2, TOK, TOK), BF),
        V((HALF, HD), BF),
        V((2, HALF, TOK), BF),
        V((8, TOK, TOK), BF),
        V((8, 2, HALF, HD), F32),
        V((8, 2, HALF, HD), BF),
        V((8, 2, HALF, HD), BF),
        V((2, 4, 2, HALF, HD), BF),
        V((2, 4, 2, HALF, HD), BF),
        V((NZ, 64, TOK), F32),
        V((4, 2, 64, TOK), BF),
        V((4, 2, 64, TOK), BF),
        V((3, HALF, HD), BF),
        V((2, TOK, HD), BF),
        V((3, 2, 2, TOK, HD), BF),
        S(2), S(2, 3), S(2, 3), S(2, 4), S(2, 4, 2, 2), S(1), S(8, 2),
        S(1), S(4), S(1), S(4), S(1), S(8), S(2), S(2),
        S(1), S(4), S(1), S(4),
        S(4), S(2, 2), S(1), S(4), S(1), S(4),
        S(2), S(2, 4, 2), S(1), S(8), S(2), S(4, 2), S(2, 3), S(2, 3),
        S(2, 2, 2), S(2, 2, 2),
    ]
    shape = lambda *s: jax.ShapeDtypeStruct(s, BF)
    outs = [shape(TOK, TOK)] * 4 + [shape(64, TOK)]
    held = pl.pallas_call(
        kernel,
        out_shape=outs,
        in_specs=[anywhere] * 5 + [smem],
        out_specs=[vmem] * 5,
        scratch_shapes=scratch,
        compiler_params=pltpu.CompilerParams(
            collective_id=0, has_side_effects=True, vmem_limit_bytes=56 * 1024 * 1024
        ),
        cost_estimate=pl.CostEstimate(flops=8 * 10**9, bytes_accessed=4 * 10**6, transcendentals=0),
    )(queries, key_rows, value_rows, w_out, out_grad, tile_kind)
    out, dq, dk, dv, wg = pl.pallas_call(
        copy_kernel, out_shape=outs, in_specs=[vmem] * 5, out_specs=[vmem] * 5
    )(*held)
    return out, dq, dk, dv, wg.T


def solution(mesh):
    in_specs = (
        P("ctx", "head"),
        P("ctx", "head"),
        P("ctx", "head"),
        P("head", None),
        P("ctx", "head"),
        P(),
    )
    out_specs = (
        P("ctx", "head"),
        P("ctx", "head"),
        P("ctx", "head"),
        P("ctx", "head"),
        P("head", "ctx"),
    )
    return jax.shard_map(
        on_device, mesh=mesh, in_specs=in_specs, out_specs=out_specs, check_vma=False
    )
```

```python
import functools

import jax
import jax.numpy as jnp
from jax import lax
from jax.experimental import pallas as pl
from jax.experimental.pallas import tpu as pltpu
from jax.sharding import PartitionSpec as P

HD = 128
TILE = 128
NX, NY, NZ = 4, 4, 8
TOK = 256
HALF = 512
SCALE = HD ** -0.5
EXP2_SCALE = SCALE * 1.4426950408889634
NEG = -1e30
MESH = pl.DeviceIdType.MESH
BF = jnp.bfloat16
F32 = jnp.float32
NT = (((1,), (1,)), ((), ()))
NN = (((1,), (0,)), ((), ()))
TN = (((0,), (0,)), ((), ()))


def dot(a, b, dims):
    return lax.dot_general(a, b, dims, preferred_element_type=F32)


def kernel(
    q_ref, k_ref, v_ref, w_ref, g_ref, kind_ref,
    out_ref, gq, gkv, wg_ref,
    kv, qs, dos, pst, mst, oT, dqT, mrow, lrow, aT, dof,
    w_in, g_all, w_all, dsend, gx, osend, afull, aall,
    part, sib_out, sib_in, rs_out, rs_in, wgp, wz_out, wz_in, gsend, out_vm, wg_vm,
    l_sem, a_send, a_recv, ag_send, ag_recv, sib_send, sib_recv,
    y_send, y_recv, yf_send, yf_recv, w_send, w_recv, d_send, d_recv,
    gx_send, gx_recv, gxf_send, gxf_recv,
    o_send, o_recv, ya_send, ya_recv, yaf_send, yaf_recv,
    rs_send, rs_recv, sb_send, sb_recv, wz_send, wz_recv, f_send, f_recv, g_send, g_recv,
):
    i = lax.axis_index("ctx")
    j = lax.axis_index("head")
    x, z = lax.div(i, NZ), lax.rem(i, NZ)
    y, c = lax.div(j, 2), lax.rem(j, 2)
    xc, xr = lax.div(x, 2), lax.rem(x, 2)

    def dev(x_, z_, y_, c_):
        return (x_ * NZ + z_, y_ * 2 + c_)

    def zplus(n):
        return lax.rem(z + (n + NZ), NZ)

    def xplus(n):
        return lax.rem(x + (n + NX), NX)

    def yplus(n):
        return lax.rem(y + (n + NY), NY)

    sibling = dev(x, z, y, 1 - c)

    def remote(src, dst, ss, rs, to):
        return pltpu.make_async_remote_copy(
            src_ref=src, dst_ref=dst, send_sem=ss, recv_sem=rs, device_id=to, device_id_type=MESH
        )

    def await_at(dst, sem):
        pltpu.make_async_copy(dst, dst, sem).wait()

    w_load = pltpu.make_async_copy(w_ref, w_in, l_sem.at[0])
    g_load = pltpu.make_async_copy(g_ref, g_all.at[j], l_sem.at[1])
    g_load.start()
    w_load.start()

    barrier = pltpu.get_barrier_semaphore()
    partners = []
    for dx in (2, 1, 3):
        for core in (c, 1 - c):
            partners.append(dev(xplus(dx), z, y, core))
    for dy in (2, 1, 3):
        partners.append(dev(x, z, yplus(dy), c))
    for dz in (1, -1):
        partners.append(dev(x, zplus(dz), y, c))
    partners.append(sibling)
    for to in partners:
        pl.semaphore_signal(barrier, inc=1, device_id=to, device_id_type=MESH)
    pl.semaphore_wait(barrier, len(partners))

    my_rows = pl.ds(pl.multiple_of(x * TOK, TOK), TOK)
    q_rows = pl.ds(pl.multiple_of(xr * TOK, TOK), TOK)
    half_rows = pl.ds(pl.multiple_of(c * HALF, HALF), HALF)

    def start_either(far, near, at):
        pl.when(x != 2 * c + at)(far.start)
        pl.when(x == 2 * c + at)(near.start)

    def a_copies(e, a):
        src = (k_ref, v_ref, q_ref)[a].at[:, pl.ds(e * HD, HD)]
        dst = qs.at[q_rows, :] if a == 2 else kv.at[z, a, my_rows, :]
        far = remote(src, dst, a_send.at[e, a], a_recv.at[xr, a], dev(2 * c + e, z, y, xc))
        near = pltpu.make_async_copy(src, dst, a_recv.at[xr, a])
        return far, near

    for a in range(3):
        for e in range(2):
            start_either(*a_copies(e, a), e)

    def y_copies(k, src, dst, ss, rs):
        if k == 0:
            return remote(src, dst.at[j], ss.at[0], rs.at[0], sibling)
        return remote(src, dst.at[j], ss.at[0], rs.at[k], dev(x, z, yplus(k), c))

    def y_slot(k, core):
        return yplus(-k) * 2 + core

    def y_forward(k, dst, ss, rs):
        slot = y_slot(k, c)
        return remote(dst.at[slot], dst.at[slot], ss.at[0], rs.at[k], sibling)

    for k in (1, 2, 3, 0):
        y_copies(k, g_ref, g_all, y_send, y_recv).start()

    def w_copy(k):
        to = lax.rem(j + k, 8)
        return remote(
            w_in.at[:, pl.ds(pl.multiple_of(to * TOK, TOK), TOK)], w_all.at[j],
            w_send.at[0], w_recv.at[k], (i, to),
        )

    def w_wait(k):
        await_at(w_all.at[lax.rem(j + 8 - k, 8)], w_recv.at[k])

    def piece(zs, a, r):
        return kv.at[zs, a, pl.ds(pl.multiple_of(c * HALF + r * TOK, TOK), TOK), :]

    def ag_copy(direction, dist, a, r, zs):
        ref = piece(zs, a, r)
        return remote(
            ref, ref, ag_send.at[direction, dist - 1], ag_recv.at[direction, dist - 1, a, r],
            dev(x, zplus(1 - 2 * direction), y, c),
        )

    def pair(zs, core, r):
        return kv.at[zs, :, pl.ds(pl.multiple_of(core * HALF + r * TOK, TOK), TOK), :]

    def sib_copy(t, r, zs):
        ref = pair(zs, c, r)
        return remote(ref, ref, sib_send.at[0], sib_recv.at[t, r], sibling)

    kpos = lax.broadcasted_iota(jnp.int32, (TILE, HALF), 0)
    qpos = lax.broadcasted_iota(jnp.int32, (TILE, HALF), 1) % TILE
    diff = kpos - qpos

    def block_of(half, b, zs):
        return 2 * ((2 * half + b // 2) * NZ + zs) + b % 2

    def forward_unit(zs, half):
        rows = pl.ds(pl.multiple_of(half * HALF, HALF), HALF)
        s = dot(kv[zs, 0, rows, :], qs[...], NT)
        parts = []
        for kb in range(4):
            limits = []
            for qb in range(4):
                kind = kind_ref[block_of(c, qb, z), block_of(half, kb, zs)]
                limit = jnp.where(kind == 1, 1000, jnp.where(kind == 2, 0, -1000))
                limits.append(jnp.full((1, TILE), limit, jnp.int32))
            limit = jnp.concatenate(limits, axis=1)
            parts.append(jnp.where(diff <= limit, s[kb * TILE:(kb + 1) * TILE, :], NEG))
        s = jnp.concatenate(parts, axis=0)
        old = mrow[...]
        new = jnp.maximum(old, jnp.max(s, axis=0, keepdims=True))
        alpha = jnp.exp2((old - new) * EXP2_SCALE)
        p = jnp.exp2((s - new) * EXP2_SCALE)
        lrow[...] = lrow[...] * alpha + jnp.sum(p, axis=0, keepdims=True)
        mrow[...] = new
        mst[zs, half] = new
        pb = p.astype(BF)
        pst[zs, half] = pb
        oT[...] = oT[...] * alpha + dot(kv[zs, 1, rows, :].T, pb, NN)

    mrow[...] = jnp.full(mrow.shape, NEG, F32)
    lrow[...] = jnp.zeros(lrow.shape, F32)
    oT[...] = jnp.zeros(oT.shape, F32)
    dqT[...] = jnp.zeros(dqT.shape, F32)
    for a in range(2):
        wz_in[1, a] = jnp.zeros((64, TOK), BF)

    def d_copies(e):
        src = dsend.at[:, pl.ds(e * HD, HD)]
        dst = dos.at[q_rows, :]
        far = remote(src, dst, d_send.at[e], d_recv.at[xr], dev(2 * c + e, z, y, xc))
        near = pltpu.make_async_copy(src, dst, d_recv.at[xr])
        return far, near

    def gx_copy(k):
        to = xplus(k)
        return remote(
            g_all.at[2 * to + c], gx.at[x, c], gx_send.at[0], gx_recv.at[k], dev(to, z, y, c)
        )

    def gx_forward(k):
        ref = gx.at[xplus(-k), c]
        return remote(ref, ref, gxf_send.at[0], gxf_recv.at[k], sibling)

    def forward_step(t, carry):
        dist = lax.div(t + 1, 2)
        odd = lax.rem(t, 2)
        zs = zplus(dist * (1 - 2 * odd))

        def arrival(e, dist):
            a, h = lax.rem(e, 2), lax.div(e, 2)
            for direction in range(2):
                r = h if direction == 0 else 1 - h
                src = zplus(dist * (2 * direction - 1))
                await_at(piece(src, a, r), ag_recv.at[direction, dist - 1, a, r])
                pl.when((dist < 3) | (h == 0))(ag_copy(direction, dist + 1, a, r, src).start)
                pl.when(a == 1)(sib_copy(2 * dist - 1 + direction, r, src).start)

        def slot(s):
            e = s + 1

            @pl.when((s > 2) & (s < 11))
            def _():
                arrival(lax.rem(e, 4), lax.div(e, 4) + 1)

        @pl.when(t == 0)
        def _():
            for a in range(2):
                for r in range(2):
                    await_at(piece(z, a, r), a_recv.at[r, a])
                    ag_copy(r, 1, a, r, z).start()
            for r in range(2):
                sib_copy(t, r, z).start()
            for a in range(2):
                for direction in range(2):
                    ag_copy(direction, 1, a, 1 - direction, z).start()
            for r in range(2):
                await_at(qs.at[pl.ds(r * TOK, TOK), :], a_recv.at[r, 2])

        @pl.when(t == 1)
        def _():
            for e in range(4):
                arrival(jnp.int32(e), jnp.int32(1))

        @pl.when(t == 7)
        def _():
            for r in range(2):
                for a in range(2):
                    await_at(piece(zs, a, r), ag_recv.at[r, 3, a, r])
                sib_copy(t, r, zs).start()

        slot(2 * t)

        @pl.when(t == 1)
        def _():
            for k in (1, 2, 3):
                await_at(g_all.at[y_slot(k, c)], y_recv.at[k])
                y_forward(k, g_all, yf_send, yf_recv).start()
            g_load.wait()
            w_load.wait()

        @pl.when(t == 2)
        def _():
            await_at(g_all.at[y * 2 + 1 - c], y_recv.at[0])
            for k in (1, 2, 3):
                await_at(g_all.at[y_slot(k, 1 - c)], yf_recv.at[k])
            d = jnp.zeros((TOK, TOK), F32)
            for h in range(8):
                d = d + dot(g_all[h], w_in[:, h * TOK:(h + 1) * TOK], NT)
            dsend[...] = d.astype(BF)
            for e in range(2):
                start_either(*d_copies(e), e)
            for k in range(1, NX):
                gx_copy(k).start()

        @pl.when(t == 3)
        def _():
            for k in range(1, 8):
                w_copy(k).start()
            for h in range(2):
                gx[x, h] = g_all[2 * x + h]
            w_all[j] = w_in[:, pl.ds(pl.multiple_of(j * TOK, TOK), TOK)]

        @pl.when(t == 6)
        def _():
            for r in range(2):
                await_at(dos.at[pl.ds(r * TOK, TOK), :], d_recv.at[r])
            dof[...] = dos[...].astype(F32).T

        forward_unit(zs, c)
        slot(2 * t + 1)
        for r in range(2):
            await_at(pair(zs, 1 - c, r), sib_recv.at[t, r])
        forward_unit(zs, 1 - c)
        return carry

    lax.fori_loop(0, 8, forward_step, 0)

    inv = 1.0 / lrow[...]
    attnT = (oT[...] * inv).astype(BF).astype(F32)
    aT[...] = attnT

    def o_copies(k):
        dst = afull.at[c, :, pl.ds(pl.multiple_of(xr * HD, HD), HD)]
        far = remote(osend, dst, o_send.at[k], o_recv.at[xr, c], dev(xplus(k), z, y, xc))
        near = pltpu.make_async_copy(osend, dst, o_recv.at[xr, c])
        return far, near

    def sb_copy(u):
        return remote(sib_out.at[u], sib_in.at[u], sb_send.at[0], sb_recv.at[u], sibling)

    def sb_wait(u):
        await_at(sib_in.at[u], sb_recv.at[u])

    def rs_copy(direction, dist, a):
        return remote(
            rs_out.at[direction, dist - 1, a], rs_in.at[direction, dist - 1, a],
            rs_send.at[0 if dist == 4 else 1], rs_recv.at[direction, dist - 1, a],
            dev(x, zplus(1 - 2 * direction), y, c),
        )

    def g_copy(direction, r, a):
        return remote(
            rs_out.at[direction, 0, a, pl.ds(r * TOK, TOK), :], gkv.at[direction, xr, a],
            g_send.at[direction, r, a], g_recv.at[direction, xr, a],
            dev(2 * c + r, zplus(1 - 2 * direction), y, xc),
        )

    def total(u, a):
        return part[u, a] + sib_in[u, a].astype(F32)

    def ring(direction, dist, a):
        value = total(0 if dist == 4 else 7 - 2 * dist + direction, a)
        if dist < 3 or (dist == 3 and a == direction):
            await_at(rs_in.at[direction, dist, a], rs_recv.at[direction, dist, a])
            value = value + rs_in[direction, dist, a].astype(F32)
        rs_out[direction, dist - 1, a] = value.astype(BF)
        if dist > 1:
            rs_copy(direction, dist, a).start()
        else:
            for r in range(2):
                g_copy(direction, r, a).start()

    def wz_copy(kind, direction):
        src, dst = wz_out.at[kind, direction], wz_in.at[kind, direction]
        if kind == 1:
            rows = pl.ds(32 * direction, 32)
            src, dst = src.at[rows, :], dst.at[rows, :]
        far = (1, 2, 1, 2)[kind] * (1 - 2 * direction)
        return remote(
            src, dst, wz_send.at[0 if kind == 1 else 1], wz_recv.at[kind, direction],
            dev(x, zplus(far), y, c),
        )

    def wz_wait(kind, direction):
        dst = wz_in.at[kind, direction]
        if kind == 1:
            dst = dst.at[pl.ds(32 * direction, 32), :]
        await_at(dst, wz_recv.at[kind, direction])

    def wz_start():
        for kind in (1, 0, 2):
            for direction in range(2):
                to = zplus((3, 4, 1)[kind] * (1 - 2 * direction))
                wz_out[kind, direction] = wgp[to].astype(BF)
                wz_copy(kind, direction).start()

    def wz_middle():
        for direction in range(2):
            for kind in (1, 0):
                wz_wait(kind, direction)
            value = wgp[zplus(2 - 4 * direction)]
            value = value + wz_in[0, direction].astype(F32) + wz_in[1, direction].astype(F32)
            wz_out[3, direction] = value.astype(BF)
            wz_copy(3, direction).start()

    def backward_unit(zs, half):
        rows = pl.ds(pl.multiple_of(half * HALF, HALF), HALF)
        dk = dv = None
        for side in range(2):
            cols = slice(side * TOK, (side + 1) * TOK)
            factor = jnp.exp2((mst[zs, half, :, cols] - mrow[:, cols]) * EXP2_SCALE) / lrow[:, cols]
            dob = (dof[:, cols] * factor).astype(BF)
            delta = jnp.sum(dob.astype(F32) * aT[:, cols], axis=0, keepdims=True)
            p = pst[zs, half, :, cols]
            dv_side = dot(p, dob, NT)
            dp = dot(kv[zs, 1, rows, :], dob, NN)
            ds = (p.astype(F32) * (dp - delta)).astype(BF)
            pst[zs, half, :, cols] = ds
            dk_side = dot(ds, qs[cols, :], NN)
            dk = dk_side if side == 0 else dk + dk_side
            dv = dv_side if side == 0 else dv + dv_side
        return dk * SCALE, dv

    def query_step(zs, carry):
        both = dot(kv[zs, 0, :HALF, :].T, pst[zs, 0], NN)
        dqT[...] += both + dot(kv[zs, 0, HALF:, :].T, pst[zs, 1], NN)
        return carry

    own_attn = afull.at[xc, q_rows, :]

    def f_copies(r, a):
        src = gsend.at[a, pl.ds(r * TOK, TOK), :]
        dst = gkv.at[2, xr, a] if a < 2 else gq.at[xr]
        far = remote(src, dst, f_send.at[r, a], f_recv.at[xr, a], dev(2 * c + r, z, y, xc))
        near = pltpu.make_async_copy(src, dst, f_recv.at[xr, a])
        return far, near

    def backward_step(n, carry):
        u = jnp.where(n == 5, 7, jnp.where(n > 5, n - 1, n))
        dist = lax.div(8 - u, 2)
        odd = lax.rem(u, 2)
        zs = zplus(dist * (2 * odd - 1))
        dk, dv = backward_unit(zs, 1 - c)
        sib_out[u, 0] = dk.astype(BF)
        sib_out[u, 1] = dv.astype(BF)
        sb_copy(u).start()
        dk, dv = backward_unit(zs, c)
        part[u, 0] = dk
        part[u, 1] = dv

        @pl.when(u == 0)
        def _():
            osend[...] = aT[...].T.astype(BF)
            for k in range(NX):
                far, near = o_copies(k)
                if k:
                    far.start()
                else:
                    pl.when(c != xc)(far.start)
                    pl.when(c == xc)(near.start)
            sb_wait(0)
            for a in range(2):
                ring(a, 4, a)

        @pl.when(u == 1)
        def _():
            sb_wait(1)
            ring(0, 3, 1)

        @pl.when(u == 2)
        def _():
            sb_wait(2)
            ring(1, 3, 0)
            for k in range(1, NX):
                await_at(gx.at[xplus(-k), c], gx_recv.at[k])
                gx_forward(k).start()

        @pl.when(u == 3)
        def _():
            for direction in range(2):
                ring(direction, 3, direction)

        @pl.when(u == 7)
        def _():
            sb_wait(3)
            sb_wait(4)
            for direction in range(2):
                ring(direction, 2, 1 - direction)
            sb_wait(7)
            for a in range(2):
                gsend[a] = total(7, a).astype(BF)
                for r in range(2):
                    start_either(*f_copies(r, a), r)
            for e in range(2):
                for half in range(2):
                    await_at(afull.at[half, :, pl.ds(e * HD, HD)], o_recv.at[e, half])
            for k in (1, 2, 3, 0):
                y_copies(k, own_attn, aall, ya_send, ya_recv).start()
            for k in range(1, NX):
                await_at(gx.at[xplus(-k), 1 - c], gxf_recv.at[k])
            for h in range(2):
                wg = jnp.zeros((TOK, TOK), F32)
                for xx in range(NX):
                    at = afull[xx // 2, (xx % 2) * TOK:(xx % 2 + 1) * TOK, :]
                    wg = wg + dot(gx[xx, h], at, TN)
                for n in range(4):
                    wgp[4 * h + n] = wg[n * 64:(n + 1) * 64, :]
            wz_start()
            aall[j] = own_attn[...]

        @pl.when(u == 5)
        def _():
            for direction in range(2):
                ring(direction, 2, direction)

        return carry

    lax.fori_loop(0, 8, backward_step, 0)

    lax.fori_loop(0, 4, query_step, 0)
    sb_wait(5)
    sb_wait(6)
    for direction in range(2):
        ring(direction, 1, 1 - direction)
    wz_middle()
    lax.fori_loop(4, 8, query_step, 0)
    gsend[2] = (dqT[...] * SCALE).T.astype(BF)
    for r in range(2):
        start_either(*f_copies(r, 2), r)
    for direction in range(2):
        ring(direction, 1, direction)
    for k in (1, 2, 3):
        await_at(aall.at[y_slot(k, c)], ya_recv.at[k])
        y_forward(k, aall, yaf_send, yaf_recv).start()

    for k in range(1, 8):
        w_wait(k)
    await_at(aall.at[y * 2 + 1 - c], ya_recv.at[0])
    for k in (1, 2, 3):
        await_at(aall.at[y_slot(k, 1 - c)], yaf_recv.at[k])
    o = jnp.zeros((TOK, TOK), F32)
    for h in range(8):
        o = o + dot(aall[h], w_all[h], NN)
    out_vm[...] = o.astype(BF)
    out_store = pltpu.make_async_copy(out_vm, out_ref, l_sem.at[2])
    out_store.start()

    for e in range(2):
        for a in range(3):
            far, _ = a_copies(e, a)
            pl.when(x != 2 * c + e)(far.wait_send)
            far, _ = f_copies(e, a)
            pl.when(x != 2 * c + e)(far.wait_send)
        far, _ = d_copies(e)
        pl.when(x != 2 * c + e)(far.wait_send)
    far, _ = o_copies(0)
    pl.when(c != xc)(far.wait_send)
    for k in range(1, NX):
        far, _ = o_copies(k)
        far.wait_send()

    def left(ref, sem):
        remote(ref, ref, sem, sem, sibling).wait_send()

    left(g_all.at[pl.ds(0, 4)], y_send.at[0])
    left(g_all.at[pl.ds(0, 4)], ya_send.at[0])
    for sem in (yf_send, yaf_send, gx_send, gxf_send):
        left(g_all.at[pl.ds(0, 3)], sem.at[0])
    left(w_all.at[pl.ds(0, 7)], w_send.at[0])
    left(sib_out, sb_send.at[0])
    left(kv.at[:, :, pl.ds(0, HALF), :], sib_send.at[0])
    left(rs_out.at[0, 3], rs_send.at[0])
    left(rs_out.at[:, pl.ds(1, 2)], rs_send.at[1])
    for direction in range(2):
        for dist in range(1, 4):
            left(kv.at[0, :, pl.ds(0, HALF), :], ag_send.at[direction, dist - 1])
        left(kv.at[0, 0, pl.ds(0, HALF), :], ag_send.at[direction, 3])

    wg = wgp[z]
    for kind in (2, 3):
        for direction in range(2):
            wz_wait(kind, direction)
            wg = wg + wz_in[kind, direction].astype(F32)
    wg_vm[...] = wg.astype(BF)
    wg_store = pltpu.make_async_copy(wg_vm, wg_ref, l_sem.at[3])
    wg_store.start()
    left(wz_out.at[0, 0], wz_send.at[0])
    left(wz_out.at[pl.ds(0, 3)], wz_send.at[1])

    for e in range(2):
        await_at(gq.at[e], f_recv.at[e, 2])
        for a in range(2):
            await_at(gkv.at[2, e, a], f_recv.at[e, a])
    out_store.wait()
    wg_store.wait()
    for direction in range(2):
        for r in range(2):
            for a in range(2):
                g_copy(direction, r, a).wait_send()
    for a in range(2):
        for e in range(2):
            for direction in range(2):
                await_at(gkv.at[direction, e, a], g_recv.at[direction, e, a])


def last_kernel(held_out, gq, gkv, held_wg, out_ref, dq_ref, dk_ref, dv_ref, wg_ref):
    out_ref[...] = held_out[...]
    wg_ref[...] = held_wg[...]
    for e in range(2):
        cols = slice(e * HD, (e + 1) * HD)
        dq_ref[:, cols] = gq[e]
        for a, ref in ((0, dk_ref), (1, dv_ref)):
            value = gkv[0, e, a].astype(F32) + gkv[1, e, a].astype(F32) + gkv[2, e, a].astype(F32)
            ref[:, cols] = value.astype(BF)


def on_device(queries, key_rows, value_rows, w_out, out_grad, tile_kind):
    vmem = pl.BlockSpec(memory_space=pltpu.VMEM)
    smem = pl.BlockSpec(memory_space=pltpu.SMEM)
    anywhere = pl.BlockSpec(memory_space=pl.ANY)
    V = pltpu.VMEM
    S = lambda *shape: pltpu.SemaphoreType.DMA(shape)
    scratch = [
        V((NZ, 2, 2 * HALF, HD), BF),
        V((HALF, HD), BF),
        V((HALF, HD), BF),
        V((NZ, 2, HALF, HALF), BF),
        V((NZ, 2, 1, HALF), F32),
        V((HD, HALF), F32),
        V((HD, HALF), F32),
        V((1, HALF), F32),
        V((1, HALF), F32),
        V((HD, HALF), F32),
        V((HD, HALF), F32),
        V((TOK, 8 * TOK), BF),
        V((8, TOK, TOK), BF),
        V((8, TOK, TOK), BF),
        V((TOK, TOK), BF),
        V((NX, 2, TOK, TOK), BF),
        V((HALF, HD), BF),
        V((2, HALF, TOK), BF),
        V((8, TOK, TOK), BF),
        V((8, 2, HALF, HD), F32),
        V((8, 2, HALF, HD), BF),
        V((8, 2, HALF, HD), BF),
        V((2, 4, 2, HALF, HD), BF),
        V((2, 4, 2, HALF, HD), BF),
        V((NZ, 64, TOK), F32),
        V((4, 2, 64, TOK), BF),
        V((4, 2, 64, TOK), BF),
        V((3, HALF, HD), BF),
        V((TOK, TOK), BF),
        V((64, TOK), BF),
        S(4), S(2, 3), S(2, 3), S(2, 4), S(2, 4, 2, 2), S(1), S(8, 2),
        S(1), S(4), S(1), S(4), S(1), S(8), S(2), S(2),
        S(1), S(4), S(1), S(4),
        S(4), S(2, 2), S(1), S(4), S(1), S(4),
        S(2), S(2, 4, 2), S(1), S(8), S(2), S(4, 2), S(2, 3), S(2, 3),
        S(2, 2, 2), S(2, 2, 2),
    ]
    shape = lambda *s: jax.ShapeDtypeStruct(s, BF)
    outs = [shape(TOK, TOK)] * 4 + [shape(64, TOK)]
    held = pl.pallas_call(
        kernel,
        out_shape=[shape(TOK, TOK), shape(2, TOK, HD), shape(3, 2, 2, TOK, HD), shape(64, TOK)],
        in_specs=[anywhere] * 5 + [smem],
        out_specs=[anywhere] * 4,
        scratch_shapes=scratch,
        compiler_params=pltpu.CompilerParams(
            collective_id=0, has_side_effects=True, vmem_limit_bytes=56 * 1024 * 1024
        ),
        cost_estimate=pl.CostEstimate(flops=8 * 10**9, bytes_accessed=4 * 10**6, transcendentals=0),
    )(queries, key_rows, value_rows, w_out, out_grad, tile_kind)
    out, dq, dk, dv, wg = pl.pallas_call(
        last_kernel, out_shape=outs, in_specs=[vmem] * 4, out_specs=[vmem] * 5
    )(*held)
    return out, dq, dk, dv, wg.T


def solution(mesh):
    in_specs = (
        P("ctx", "head"),
        P("ctx", "head"),
        P("ctx", "head"),
        P("head", None),
        P("ctx", "head"),
        P(),
    )
    out_specs = (
        P("ctx", "head"),
        P("ctx", "head"),
        P("ctx", "head"),
        P("ctx", "head"),
        P("head", "ctx"),
    )
    return jax.shard_map(
        on_device, mesh=mesh, in_specs=in_specs, out_specs=out_specs, check_vma=False
    )
```

```python
import functools

import jax
import jax.numpy as jnp
from jax import lax
from jax.experimental import pallas as pl
from jax.experimental.pallas import tpu as pltpu
from jax.sharding import PartitionSpec as P

HD = 128
TILE = 128
NX, NY, NZ = 4, 4, 8
TOK = 256
HALF = 512
SCALE = HD ** -0.5
EXP2_SCALE = SCALE * 1.4426950408889634
NEG = -1e30
MESH = pl.DeviceIdType.MESH
BF = jnp.bfloat16
F32 = jnp.float32
NT = (((1,), (1,)), ((), ()))
NN = (((1,), (0,)), ((), ()))
TN = (((0,), (0,)), ((), ()))


def dot(a, b, dims):
    return lax.dot_general(a, b, dims, preferred_element_type=F32)


def kernel(
    q_ref, k_ref, v_ref, w_ref, g_ref, kind_ref,
    out_ref, gq, gkv, wg_ref,
    kv, qs, dos, pst, mst, oT, dqT, mrow, lrow, aT, dof, delta,
    w_in, g_all, w_all, dsend, gx, osend, afull, aall,
    part, sib_out, sib_in, rs_out, rs_in, wgp, wz_out, wz_in, gsend, out_vm, wg_vm,
    l_sem, a_send, a_recv, ag_send, ag_recv, sib_send, sib_recv,
    y_send, y_recv, yf_send, yf_recv, w_send, w_recv, d_send, d_recv,
    gx_send, gx_recv, gxf_send, gxf_recv,
    o_send, o_recv, ya_send, ya_recv, yaf_send, yaf_recv,
    rs_send, rs_recv, sb_send, sb_recv, wz_send, wz_recv, f_send, f_recv, g_send, g_recv,
):
    i = lax.axis_index("ctx")
    j = lax.axis_index("head")
    x, z = lax.div(i, NZ), lax.rem(i, NZ)
    y, c = lax.div(j, 2), lax.rem(j, 2)
    xc, xr = lax.div(x, 2), lax.rem(x, 2)

    def dev(x_, z_, y_, c_):
        return (x_ * NZ + z_, y_ * 2 + c_)

    def zplus(n):
        return lax.rem(z + (n + NZ), NZ)

    def xplus(n):
        return lax.rem(x + (n + NX), NX)

    def yplus(n):
        return lax.rem(y + (n + NY), NY)

    sibling = dev(x, z, y, 1 - c)

    def remote(src, dst, ss, rs, to):
        return pltpu.make_async_remote_copy(
            src_ref=src, dst_ref=dst, send_sem=ss, recv_sem=rs, device_id=to, device_id_type=MESH
        )

    def await_at(dst, sem):
        pltpu.make_async_copy(dst, dst, sem).wait()

    w_load = pltpu.make_async_copy(w_ref, w_in, l_sem.at[0])
    g_load = pltpu.make_async_copy(g_ref, g_all.at[j], l_sem.at[1])
    g_load.start()
    w_load.start()

    barrier = pltpu.get_barrier_semaphore()
    partners = []
    for dx in (2, 1, 3):
        for core in (c, 1 - c):
            partners.append(dev(xplus(dx), z, y, core))
    for dy in (2, 1, 3):
        partners.append(dev(x, z, yplus(dy), c))
    for dz in (1, -1):
        partners.append(dev(x, zplus(dz), y, c))
    partners.append(sibling)
    for to in partners:
        pl.semaphore_signal(barrier, inc=1, device_id=to, device_id_type=MESH)
    pl.semaphore_wait(barrier, len(partners))

    my_rows = pl.ds(pl.multiple_of(x * TOK, TOK), TOK)
    q_rows = pl.ds(pl.multiple_of(xr * TOK, TOK), TOK)
    half_rows = pl.ds(pl.multiple_of(c * HALF, HALF), HALF)

    def start_either(far, near, at):
        pl.when(x != 2 * c + at)(far.start)
        pl.when(x == 2 * c + at)(near.start)

    def a_copies(e, a):
        src = (k_ref, v_ref, q_ref)[a].at[:, pl.ds(e * HD, HD)]
        dst = qs.at[q_rows, :] if a == 2 else kv.at[z, a, my_rows, :]
        far = remote(src, dst, a_send.at[e, a], a_recv.at[xr, a], dev(2 * c + e, z, y, xc))
        near = pltpu.make_async_copy(src, dst, a_recv.at[xr, a])
        return far, near

    for a in range(3):
        for e in range(2):
            start_either(*a_copies(e, a), e)

    def y_copies(k, src, dst, ss, rs):
        if k == 0:
            return remote(src, dst.at[j], ss.at[0], rs.at[0], sibling)
        return remote(src, dst.at[j], ss.at[0], rs.at[k], dev(x, z, yplus(k), c))

    def y_slot(k, core):
        return yplus(-k) * 2 + core

    def y_forward(k, dst, ss, rs):
        slot = y_slot(k, c)
        return remote(dst.at[slot], dst.at[slot], ss.at[0], rs.at[k], sibling)

    for k in (1, 2, 3, 0):
        y_copies(k, g_ref, g_all, y_send, y_recv).start()

    def w_copy(k):
        to = lax.rem(j + k, 8)
        return remote(
            w_in.at[:, pl.ds(pl.multiple_of(to * TOK, TOK), TOK)], w_all.at[j],
            w_send.at[0], w_recv.at[k], (i, to),
        )

    def w_wait(k):
        await_at(w_all.at[lax.rem(j + 8 - k, 8)], w_recv.at[k])

    def piece(zs, a, r):
        return kv.at[zs, a, pl.ds(pl.multiple_of(c * HALF + r * TOK, TOK), TOK), :]

    def ag_copy(direction, dist, a, r, zs):
        ref = piece(zs, a, r)
        return remote(
            ref, ref, ag_send.at[direction, dist - 1], ag_recv.at[direction, dist - 1, a, r],
            dev(x, zplus(1 - 2 * direction), y, c),
        )

    def pair(zs, core, r):
        return kv.at[zs, :, pl.ds(pl.multiple_of(core * HALF + r * TOK, TOK), TOK), :]

    def sib_copy(t, r, zs):
        ref = pair(zs, c, r)
        return remote(ref, ref, sib_send.at[0], sib_recv.at[t, r], sibling)

    kpos = lax.broadcasted_iota(jnp.int32, (TILE, HALF), 0)
    qpos = lax.broadcasted_iota(jnp.int32, (TILE, HALF), 1) % TILE
    diff = kpos - qpos

    def block_of(half, b, zs):
        return 2 * ((2 * half + b // 2) * NZ + zs) + b % 2

    def forward_unit(zs, half):
        rows = pl.ds(pl.multiple_of(half * HALF, HALF), HALF)
        s = dot(kv[zs, 0, rows, :], qs[...], NT)
        parts = []
        for kb in range(4):
            limits = []
            for qb in range(4):
                kind = kind_ref[block_of(c, qb, z), block_of(half, kb, zs)]
                limit = jnp.where(kind == 1, 1000, jnp.where(kind == 2, 0, -1000))
                limits.append(jnp.full((1, TILE), limit, jnp.int32))
            limit = jnp.concatenate(limits, axis=1)
            parts.append(jnp.where(diff <= limit, s[kb * TILE:(kb + 1) * TILE, :], NEG))
        s = jnp.concatenate(parts, axis=0)
        old = mrow[...]
        new = jnp.maximum(old, jnp.max(s, axis=0, keepdims=True))
        alpha = jnp.exp2((old - new) * EXP2_SCALE)
        p = jnp.exp2((s - new) * EXP2_SCALE)
        lrow[...] = lrow[...] * alpha + jnp.sum(p, axis=0, keepdims=True)
        mrow[...] = new
        mst[zs, half] = new
        pb = p.astype(BF)
        pst[zs, half] = pb
        oT[...] = oT[...] * alpha + dot(kv[zs, 1, rows, :].T, pb, NN)

    mrow[...] = jnp.full(mrow.shape, NEG, F32)
    lrow[...] = jnp.zeros(lrow.shape, F32)
    oT[...] = jnp.zeros(oT.shape, F32)
    dqT[...] = jnp.zeros(dqT.shape, F32)
    for a in range(2):
        wz_in[1, a] = jnp.zeros((64, TOK), BF)

    def d_copies(e):
        src = dsend.at[:, pl.ds(e * HD, HD)]
        dst = dos.at[q_rows, :]
        far = remote(src, dst, d_send.at[e], d_recv.at[xr], dev(2 * c + e, z, y, xc))
        near = pltpu.make_async_copy(src, dst, d_recv.at[xr])
        return far, near

    def gx_copy(k):
        to = xplus(k)
        return remote(
            g_all.at[2 * to + c], gx.at[x, c], gx_send.at[0], gx_recv.at[k], dev(to, z, y, c)
        )

    def gx_forward(k):
        ref = gx.at[xplus(-k), c]
        return remote(ref, ref, gxf_send.at[0], gxf_recv.at[k], sibling)

    def chunk_of(t):
        return zplus(lax.div(t + 1, 2) * (1 - 2 * lax.rem(t, 2)))

    def forward_step(t, carry):
        dist = lax.div(t + 1, 2)
        zs = chunk_of(t)

        def arrival(e, dist):
            a, h = lax.rem(e, 2), lax.div(e, 2)
            for direction in range(2):
                r = h if direction == 0 else 1 - h
                src = zplus(dist * (2 * direction - 1))
                await_at(piece(src, a, r), ag_recv.at[direction, dist - 1, a, r])
                pl.when((dist < 3) | (h == 0))(ag_copy(direction, dist + 1, a, r, src).start)
                pl.when(a == 1)(sib_copy(2 * dist - 1 + direction, r, src).start)

        def slot(s):
            e = s + 1

            @pl.when((s > 2) & (s < 11))
            def _():
                arrival(lax.rem(e, 4), lax.div(e, 4) + 1)

        @pl.when(t == 0)
        def _():
            for a in range(2):
                for r in range(2):
                    await_at(piece(z, a, r), a_recv.at[r, a])
                    ag_copy(r, 1, a, r, z).start()
            for r in range(2):
                sib_copy(t, r, z).start()
            for a in range(2):
                for direction in range(2):
                    ag_copy(direction, 1, a, 1 - direction, z).start()
            for r in range(2):
                await_at(qs.at[pl.ds(r * TOK, TOK), :], a_recv.at[r, 2])

        @pl.when(t == 1)
        def _():
            for e in range(4):
                arrival(jnp.int32(e), jnp.int32(1))

        @pl.when(t == 7)
        def _():
            for r in range(2):
                for a in range(2):
                    await_at(piece(zs, a, r), ag_recv.at[r, 3, a, r])
                sib_copy(t, r, zs).start()

        slot(2 * t)

        @pl.when(t == 1)
        def _():
            for k in (1, 2, 3):
                await_at(g_all.at[y_slot(k, c)], y_recv.at[k])
                y_forward(k, g_all, yf_send, yf_recv).start()
            g_load.wait()
            w_load.wait()

        @pl.when(t == 2)
        def _():
            await_at(g_all.at[y * 2 + 1 - c], y_recv.at[0])
            for k in (1, 2, 3):
                await_at(g_all.at[y_slot(k, 1 - c)], yf_recv.at[k])
            d = jnp.zeros((TOK, TOK), F32)
            for h in range(8):
                d = d + dot(g_all[h], w_in[:, h * TOK:(h + 1) * TOK], NT)
            dsend[...] = d.astype(BF)
            for e in range(2):
                start_either(*d_copies(e), e)
            for k in range(1, NX):
                gx_copy(k).start()

        @pl.when(t == 3)
        def _():
            for k in range(1, 8):
                w_copy(k).start()
            for h in range(2):
                gx[x, h] = g_all[2 * x + h]
            w_all[j] = w_in[:, pl.ds(pl.multiple_of(j * TOK, TOK), TOK)]

        forward_unit(zs, c)
        slot(2 * t + 1)
        for r in range(2):
            await_at(pair(zs, 1 - c, r), sib_recv.at[t, r])
        forward_unit(zs, 1 - c)

        @pl.when(t == 6)
        def _():
            for r in range(2):
                await_at(dos.at[pl.ds(r * TOK, TOK), :], d_recv.at[r])
            dof[...] = dos[...].astype(F32).T

        return carry

    lax.fori_loop(0, 8, forward_step, 0)

    inv = 1.0 / lrow[...]
    attnT = (oT[...] * inv).astype(BF).astype(F32)
    aT[...] = attnT
    delta[...] = jnp.sum(dof[...] * attnT, axis=0, keepdims=True)

    def o_copies(k):
        dst = afull.at[c, :, pl.ds(pl.multiple_of(xr * HD, HD), HD)]
        far = remote(osend, dst, o_send.at[k], o_recv.at[xr, c], dev(xplus(k), z, y, xc))
        near = pltpu.make_async_copy(osend, dst, o_recv.at[xr, c])
        return far, near

    def sb_copy(u):
        return remote(sib_out.at[u], sib_in.at[u], sb_send.at[0], sb_recv.at[u], sibling)

    def sb_wait(u):
        await_at(sib_in.at[u], sb_recv.at[u])

    def rs_copy(direction, dist, a):
        return remote(
            rs_out.at[direction, dist - 1, a], rs_in.at[direction, dist - 1, a],
            rs_send.at[0 if dist == 4 else 1], rs_recv.at[direction, dist - 1, a],
            dev(x, zplus(1 - 2 * direction), y, c),
        )

    def g_copy(direction, r, a):
        return remote(
            rs_out.at[direction, 0, a, pl.ds(r * TOK, TOK), :], gkv.at[direction, xr, a],
            g_send.at[direction, r, a], g_recv.at[direction, xr, a],
            dev(2 * c + r, zplus(1 - 2 * direction), y, xc),
        )

    def total(u, a):
        return part[u, a] + sib_in[u, a].astype(F32)

    def ring(direction, dist, a):
        value = total(0 if dist == 4 else 7 - 2 * dist + direction, a)
        if dist < 3 or (dist == 3 and a == direction):
            await_at(rs_in.at[direction, dist, a], rs_recv.at[direction, dist, a])
            value = value + rs_in[direction, dist, a].astype(F32)
        rs_out[direction, dist - 1, a] = value.astype(BF)
        if dist > 1:
            rs_copy(direction, dist, a).start()
        else:
            for r in range(2):
                g_copy(direction, r, a).start()

    def wz_copy(kind, direction):
        src, dst = wz_out.at[kind, direction], wz_in.at[kind, direction]
        if kind == 1:
            rows = pl.ds(32 * direction, 32)
            src, dst = src.at[rows, :], dst.at[rows, :]
        far = (1, 2, 1, 2)[kind] * (1 - 2 * direction)
        return remote(
            src, dst, wz_send.at[0 if kind == 1 else 1], wz_recv.at[kind, direction],
            dev(x, zplus(far), y, c),
        )

    def wz_wait(kind, direction):
        dst = wz_in.at[kind, direction]
        if kind == 1:
            dst = dst.at[pl.ds(32 * direction, 32), :]
        await_at(dst, wz_recv.at[kind, direction])

    def wz_start():
        for kind in (1, 0, 2):
            for direction in range(2):
                to = zplus((3, 4, 1)[kind] * (1 - 2 * direction))
                wz_out[kind, direction] = wgp[to].astype(BF)
                wz_copy(kind, direction).start()

    def wz_middle():
        for direction in range(2):
            for kind in (1, 0):
                wz_wait(kind, direction)
            value = wgp[zplus(2 - 4 * direction)]
            value = value + wz_in[0, direction].astype(F32) + wz_in[1, direction].astype(F32)
            wz_out[3, direction] = value.astype(BF)
            wz_copy(3, direction).start()

    def backward_unit(zs, half):
        rows = pl.ds(pl.multiple_of(half * HALF, HALF), HALF)
        dk = dv = None
        for side in range(2):
            cols = slice(side * TOK, (side + 1) * TOK)
            factor = jnp.exp2((mst[zs, half, :, cols] - mrow[:, cols]) * EXP2_SCALE) / lrow[:, cols]
            p = pst[zs, half, :, cols].astype(F32) * factor
            dp = dot(kv[zs, 1, rows, :], dos[cols, :], NT)
            ds = (p * (dp - delta[:, cols])).astype(BF)
            dv_side = dot(p.astype(BF), dos[cols, :], NN)
            pst[zs, half, :, cols] = ds
            dk_side = dot(ds, qs[cols, :], NN)
            dk = dk_side if side == 0 else dk + dk_side
            dv = dv_side if side == 0 else dv + dv_side
        return dk * SCALE, dv

    def query_step(zs, carry):
        both = dot(kv[zs, 0, :HALF, :].T, pst[zs, 0], NN)
        dqT[...] += both + dot(kv[zs, 0, HALF:, :].T, pst[zs, 1], NN)
        return carry

    own_attn = afull.at[xc, q_rows, :]

    def f_copies(r, a):
        src = gsend.at[a, pl.ds(r * TOK, TOK), :]
        dst = gkv.at[2, xr, a] if a < 2 else gq.at[xr]
        far = remote(src, dst, f_send.at[r, a], f_recv.at[xr, a], dev(2 * c + r, z, y, xc))
        near = pltpu.make_async_copy(src, dst, f_recv.at[xr, a])
        return far, near

    def backward_step(n, carry):
        u = jnp.where(n == 5, 7, jnp.where(n > 5, n - 1, n))
        dist = lax.div(8 - u, 2)
        odd = lax.rem(u, 2)
        zs = zplus(dist * (2 * odd - 1))
        dk, dv = backward_unit(zs, 1 - c)
        sib_out[u, 0] = dk.astype(BF)
        sib_out[u, 1] = dv.astype(BF)
        sb_copy(u).start()
        dk, dv = backward_unit(zs, c)
        part[u, 0] = dk
        part[u, 1] = dv

        @pl.when(u == 0)
        def _():
            osend[...] = aT[...].T.astype(BF)
            for k in range(NX):
                far, near = o_copies(k)
                if k:
                    far.start()
                else:
                    pl.when(c != xc)(far.start)
                    pl.when(c == xc)(near.start)
            sb_wait(0)
            for a in range(2):
                ring(a, 4, a)

        @pl.when(u == 1)
        def _():
            sb_wait(1)
            ring(0, 3, 1)

        @pl.when(u == 2)
        def _():
            sb_wait(2)
            ring(1, 3, 0)
            for k in range(1, NX):
                await_at(gx.at[xplus(-k), c], gx_recv.at[k])
                gx_forward(k).start()

        @pl.when(u == 3)
        def _():
            for direction in range(2):
                ring(direction, 3, direction)

        @pl.when(u == 7)
        def _():
            sb_wait(3)
            sb_wait(4)
            for direction in range(2):
                ring(direction, 2, 1 - direction)
            sb_wait(7)
            for a in range(2):
                gsend[a] = total(7, a).astype(BF)
                for r in range(2):
                    start_either(*f_copies(r, a), r)
            for e in range(2):
                for half in range(2):
                    await_at(afull.at[half, :, pl.ds(e * HD, HD)], o_recv.at[e, half])
            for k in (1, 2, 3, 0):
                y_copies(k, own_attn, aall, ya_send, ya_recv).start()
            for k in range(1, NX):
                await_at(gx.at[xplus(-k), 1 - c], gxf_recv.at[k])
            for h in range(2):
                wg = jnp.zeros((TOK, TOK), F32)
                for xx in range(NX):
                    at = afull[xx // 2, (xx % 2) * TOK:(xx % 2 + 1) * TOK, :]
                    wg = wg + dot(gx[xx, h], at, TN)
                for n in range(4):
                    wgp[4 * h + n] = wg[n * 64:(n + 1) * 64, :]
            wz_start()
            aall[j] = own_attn[...]

        @pl.when(u == 5)
        def _():
            for direction in range(2):
                ring(direction, 2, direction)

        return carry

    lax.fori_loop(0, 8, backward_step, 0)

    lax.fori_loop(0, 4, query_step, 0)
    sb_wait(5)
    sb_wait(6)
    for direction in range(2):
        ring(direction, 1, 1 - direction)
    wz_middle()
    lax.fori_loop(4, 8, query_step, 0)
    gsend[2] = (dqT[...] * SCALE).T.astype(BF)
    for r in range(2):
        start_either(*f_copies(r, 2), r)
    for direction in range(2):
        ring(direction, 1, direction)
    for k in (1, 2, 3):
        await_at(aall.at[y_slot(k, c)], ya_recv.at[k])
        y_forward(k, aall, yaf_send, yaf_recv).start()

    for k in range(1, 8):
        w_wait(k)
    await_at(aall.at[y * 2 + 1 - c], ya_recv.at[0])
    for k in (1, 2, 3):
        await_at(aall.at[y_slot(k, 1 - c)], yaf_recv.at[k])
    o = jnp.zeros((TOK, TOK), F32)
    for h in range(8):
        o = o + dot(aall[h], w_all[h], NN)
    out_vm[...] = o.astype(BF)
    out_store = pltpu.make_async_copy(out_vm, out_ref, l_sem.at[2])
    out_store.start()

    for e in range(2):
        for a in range(3):
            far, _ = a_copies(e, a)
            pl.when(x != 2 * c + e)(far.wait_send)
            far, _ = f_copies(e, a)
            pl.when(x != 2 * c + e)(far.wait_send)
        far, _ = d_copies(e)
        pl.when(x != 2 * c + e)(far.wait_send)
    far, _ = o_copies(0)
    pl.when(c != xc)(far.wait_send)
    for k in range(1, NX):
        far, _ = o_copies(k)
        far.wait_send()

    def left(ref, sem):
        remote(ref, ref, sem, sem, sibling).wait_send()

    left(g_all.at[pl.ds(0, 4)], y_send.at[0])
    left(g_all.at[pl.ds(0, 4)], ya_send.at[0])
    for sem in (yf_send, yaf_send, gx_send, gxf_send):
        left(g_all.at[pl.ds(0, 3)], sem.at[0])
    left(w_all.at[pl.ds(0, 7)], w_send.at[0])
    left(sib_out, sb_send.at[0])
    left(kv.at[:, :, pl.ds(0, HALF), :], sib_send.at[0])
    left(rs_out.at[0, 3], rs_send.at[0])
    left(rs_out.at[:, pl.ds(1, 2)], rs_send.at[1])
    for direction in range(2):
        for dist in range(1, 4):
            left(kv.at[0, :, pl.ds(0, HALF), :], ag_send.at[direction, dist - 1])
        left(kv.at[0, 0, pl.ds(0, HALF), :], ag_send.at[direction, 3])

    wg = wgp[z]
    for kind in (2, 3):
        for direction in range(2):
            wz_wait(kind, direction)
            wg = wg + wz_in[kind, direction].astype(F32)
    wg_vm[...] = wg.astype(BF)
    wg_store = pltpu.make_async_copy(wg_vm, wg_ref, l_sem.at[3])
    wg_store.start()
    left(wz_out.at[0, 0], wz_send.at[0])
    left(wz_out.at[pl.ds(0, 3)], wz_send.at[1])

    for e in range(2):
        await_at(gq.at[e], f_recv.at[e, 2])
        for a in range(2):
            await_at(gkv.at[2, e, a], f_recv.at[e, a])
    out_store.wait()
    wg_store.wait()
    for direction in range(2):
        for r in range(2):
            for a in range(2):
                g_copy(direction, r, a).wait_send()
    for a in range(2):
        for e in range(2):
            for direction in range(2):
                await_at(gkv.at[direction, e, a], g_recv.at[direction, e, a])


def last_kernel(held_out, gq, gkv, held_wg, out_ref, dq_ref, dk_ref, dv_ref, wg_ref):
    out_ref[...] = held_out[...]
    wg_ref[...] = held_wg[...]
    for e in range(2):
        cols = slice(e * HD, (e + 1) * HD)
        dq_ref[:, cols] = gq[e]
        for a, ref in ((0, dk_ref), (1, dv_ref)):
            value = gkv[0, e, a].astype(F32) + gkv[1, e, a].astype(F32) + gkv[2, e, a].astype(F32)
            ref[:, cols] = value.astype(BF)


def on_device(queries, key_rows, value_rows, w_out, out_grad, tile_kind):
    vmem = pl.BlockSpec(memory_space=pltpu.VMEM)
    smem = pl.BlockSpec(memory_space=pltpu.SMEM)
    anywhere = pl.BlockSpec(memory_space=pl.ANY)
    V = pltpu.VMEM
    S = lambda *shape: pltpu.SemaphoreType.DMA(shape)
    scratch = [
        V((NZ, 2, 2 * HALF, HD), BF),
        V((HALF, HD), BF),
        V((HALF, HD), BF),
        V((NZ, 2, HALF, HALF), BF),
        V((NZ, 2, 1, HALF), F32),
        V((HD, HALF), F32),
        V((HD, HALF), F32),
        V((1, HALF), F32),
        V((1, HALF), F32),
        V((HD, HALF), F32),
        V((HD, HALF), F32),
        V((1, HALF), F32),
        V((TOK, 8 * TOK), BF),
        V((8, TOK, TOK), BF),
        V((8, TOK, TOK), BF),
        V((TOK, TOK), BF),
        V((NX, 2, TOK, TOK), BF),
        V((HALF, HD), BF),
        V((2, HALF, TOK), BF),
        V((8, TOK, TOK), BF),
        V((8, 2, HALF, HD), F32),
        V((8, 2, HALF, HD), BF),
        V((8, 2, HALF, HD), BF),
        V((2, 4, 2, HALF, HD), BF),
        V((2, 4, 2, HALF, HD), BF),
        V((NZ, 64, TOK), F32),
        V((4, 2, 64, TOK), BF),
        V((4, 2, 64, TOK), BF),
        V((3, HALF, HD), BF),
        V((TOK, TOK), BF),
        V((64, TOK), BF),
        S(4), S(2, 3), S(2, 3), S(2, 4), S(2, 4, 2, 2), S(1), S(8, 2),
        S(1), S(4), S(1), S(4), S(1), S(8), S(2), S(2),
        S(1), S(4), S(1), S(4),
        S(4), S(2, 2), S(1), S(4), S(1), S(4),
        S(2), S(2, 4, 2), S(1), S(8), S(2), S(4, 2), S(2, 3), S(2, 3),
        S(2, 2, 2), S(2, 2, 2),
    ]
    shape = lambda *s: jax.ShapeDtypeStruct(s, BF)
    outs = [shape(TOK, TOK)] * 4 + [shape(64, TOK)]
    held = pl.pallas_call(
        kernel,
        out_shape=[shape(TOK, TOK), shape(2, TOK, HD), shape(3, 2, 2, TOK, HD), shape(64, TOK)],
        in_specs=[anywhere] * 5 + [smem],
        out_specs=[anywhere] * 4,
        scratch_shapes=scratch,
        compiler_params=pltpu.CompilerParams(
            collective_id=0, has_side_effects=True, vmem_limit_bytes=56 * 1024 * 1024
        ),
        cost_estimate=pl.CostEstimate(flops=8 * 10**9, bytes_accessed=4 * 10**6, transcendentals=0),
    )(queries, key_rows, value_rows, w_out, out_grad, tile_kind)
    out, dq, dk, dv, wg = pl.pallas_call(
        last_kernel, out_shape=outs, in_specs=[vmem] * 4, out_specs=[vmem] * 5
    )(*held)
    return out, dq, dk, dv, wg.T


def solution(mesh):
    in_specs = (
        P("ctx", "head"),
        P("ctx", "head"),
        P("ctx", "head"),
        P("head", None),
        P("ctx", "head"),
        P(),
    )
    out_specs = (
        P("ctx", "head"),
        P("ctx", "head"),
        P("ctx", "head"),
        P("ctx", "head"),
        P("head", "ctx"),
    )
    return jax.shard_map(
        on_device, mesh=mesh, in_specs=in_specs, out_specs=out_specs, check_vma=False
    )
```

```python
import functools

import jax
import jax.numpy as jnp
from jax import lax
from jax.experimental import pallas as pl
from jax.experimental.pallas import tpu as pltpu
from jax.sharding import PartitionSpec as P

HD = 128
TILE = 128
NX, NY, NZ = 4, 4, 8
TOK = 256
HALF = 512
SCALE = HD ** -0.5
EXP2_SCALE = SCALE * 1.4426950408889634
NEG = -1e30
MESH = pl.DeviceIdType.MESH
BF = jnp.bfloat16
F32 = jnp.float32
NT = (((1,), (1,)), ((), ()))
NN = (((1,), (0,)), ((), ()))
TN = (((0,), (0,)), ((), ()))


def dot(a, b, dims):
    return lax.dot_general(a, b, dims, preferred_element_type=F32)


def kernel(
    q_ref, k_ref, v_ref, w_ref, g_ref, kind_ref,
    out_ref, gq, gkv, wg_ref,
    kv, qs, dos, pst, mst, oT, dqT, mrow, lrow, aT, dof, delta,
    w_in, g_all, w_all, dsend, gx, osend, afull, aall,
    part, sib_out, sib_in, rs_out, rs_in, wgp, wz_out, wz_in, gsend, out_vm, wg_vm,
    l_sem, a_send, a_recv, ag_send, ag_recv, sib_send, sib_recv,
    y_send, y_recv, yf_send, yf_recv, w_send, w_recv, d_send, d_recv,
    gx_send, gx_recv, gxf_send, gxf_recv,
    o_send, o_recv, ya_send, ya_recv, yaf_send, yaf_recv,
    rs_send, rs_recv, sb_send, sb_recv, wz_send, wz_recv, f_send, f_recv, g_send, g_recv,
):
    i = lax.axis_index("ctx")
    j = lax.axis_index("head")
    x, z = lax.div(i, NZ), lax.rem(i, NZ)
    y, c = lax.div(j, 2), lax.rem(j, 2)
    xc, xr = lax.div(x, 2), lax.rem(x, 2)

    def dev(x_, z_, y_, c_):
        return (x_ * NZ + z_, y_ * 2 + c_)

    def zplus(n):
        return lax.rem(z + (n + NZ), NZ)

    def xplus(n):
        return lax.rem(x + (n + NX), NX)

    def yplus(n):
        return lax.rem(y + (n + NY), NY)

    sibling = dev(x, z, y, 1 - c)

    def remote(src, dst, ss, rs, to):
        return pltpu.make_async_remote_copy(
            src_ref=src, dst_ref=dst, send_sem=ss, recv_sem=rs, device_id=to, device_id_type=MESH
        )

    def await_at(dst, sem):
        pltpu.make_async_copy(dst, dst, sem).wait()

    w_load = pltpu.make_async_copy(w_ref, w_in, l_sem.at[0])
    g_load = pltpu.make_async_copy(g_ref, g_all.at[j], l_sem.at[1])
    g_load.start()
    w_load.start()

    barrier = pltpu.get_barrier_semaphore()
    partners = []
    for dx in (2, 1, 3):
        for core in (c, 1 - c):
            partners.append(dev(xplus(dx), z, y, core))
    for dy in (2, 1, 3):
        partners.append(dev(x, z, yplus(dy), c))
    for dz in (1, -1):
        partners.append(dev(x, zplus(dz), y, c))
    partners.append(sibling)
    for to in partners:
        pl.semaphore_signal(barrier, inc=1, device_id=to, device_id_type=MESH)
    pl.semaphore_wait(barrier, len(partners))

    my_rows = pl.ds(pl.multiple_of(x * TOK, TOK), TOK)
    q_rows = pl.ds(pl.multiple_of(xr * TOK, TOK), TOK)
    half_rows = pl.ds(pl.multiple_of(c * HALF, HALF), HALF)

    def start_either(far, near, at):
        pl.when(x != 2 * c + at)(far.start)
        pl.when(x == 2 * c + at)(near.start)

    def a_copies(e, a):
        src = (k_ref, v_ref, q_ref)[a].at[:, pl.ds(e * HD, HD)]
        dst = qs.at[q_rows, :] if a == 2 else kv.at[z, a, my_rows, :]
        far = remote(src, dst, a_send.at[e, a], a_recv.at[xr, a], dev(2 * c + e, z, y, xc))
        near = pltpu.make_async_copy(src, dst, a_recv.at[xr, a])
        return far, near

    for a in range(3):
        for e in range(2):
            start_either(*a_copies(e, a), e)

    def y_copies(k, src, dst, ss, rs):
        if k == 0:
            return remote(src, dst.at[j], ss.at[0], rs.at[0], sibling)
        return remote(src, dst.at[j], ss.at[0], rs.at[k], dev(x, z, yplus(k), c))

    def y_slot(k, core):
        return yplus(-k) * 2 + core

    def y_forward(k, dst, ss, rs):
        slot = y_slot(k, c)
        return remote(dst.at[slot], dst.at[slot], ss.at[0], rs.at[k], sibling)

    for k in (1, 2, 3, 0):
        y_copies(k, g_ref, g_all, y_send, y_recv).start()

    def w_copy(k):
        to = lax.rem(j + k, 8)
        return remote(
            w_in.at[:, pl.ds(pl.multiple_of(to * TOK, TOK), TOK)], w_all.at[j],
            w_send.at[0], w_recv.at[k], (i, to),
        )

    def w_wait(k):
        await_at(w_all.at[lax.rem(j + 8 - k, 8)], w_recv.at[k])

    def piece(zs, a, r):
        return kv.at[zs, a, pl.ds(pl.multiple_of(c * HALF + r * TOK, TOK), TOK), :]

    def ag_copy(direction, dist, a, r, zs):
        ref = piece(zs, a, r)
        return remote(
            ref, ref, ag_send.at[direction, dist - 1], ag_recv.at[direction, dist - 1, a, r],
            dev(x, zplus(1 - 2 * direction), y, c),
        )

    def pair(zs, core, r):
        return kv.at[zs, :, pl.ds(pl.multiple_of(core * HALF + r * TOK, TOK), TOK), :]

    def sib_copy(t, r, zs):
        ref = pair(zs, c, r)
        return remote(ref, ref, sib_send.at[0], sib_recv.at[t, r], sibling)

    def last_sib_copy(a, zs):
        ref = kv.at[zs, a, half_rows, :]
        return remote(ref, ref, sib_send.at[0], sib_recv.at[7, a], sibling)

    kpos = lax.broadcasted_iota(jnp.int32, (TILE, HALF), 0)
    qpos = lax.broadcasted_iota(jnp.int32, (TILE, HALF), 1) % TILE
    diff = kpos - qpos

    def block_of(half, b, zs):
        return 2 * ((2 * half + b // 2) * NZ + zs) + b % 2

    def forward_unit(zs, half, values_wait):
        rows = pl.ds(pl.multiple_of(half * HALF, HALF), HALF)
        s = dot(kv[zs, 0, rows, :], qs[...], NT)
        parts = []
        for kb in range(4):
            limits = []
            for qb in range(4):
                kind = kind_ref[block_of(c, qb, z), block_of(half, kb, zs)]
                limit = jnp.where(kind == 1, 1000, jnp.where(kind == 2, 0, -1000))
                limits.append(jnp.full((1, TILE), limit, jnp.int32))
            limit = jnp.concatenate(limits, axis=1)
            parts.append(jnp.where(diff <= limit, s[kb * TILE:(kb + 1) * TILE, :], NEG))
        s = jnp.concatenate(parts, axis=0)
        old = mrow[...]
        new = jnp.maximum(old, jnp.max(s, axis=0, keepdims=True))
        alpha = jnp.exp2((old - new) * EXP2_SCALE)
        p = jnp.exp2((s - new) * EXP2_SCALE)
        lrow[...] = lrow[...] * alpha + jnp.sum(p, axis=0, keepdims=True)
        mrow[...] = new
        mst[zs, half] = new
        pst[zs, half] = p.astype(BF)
        values_wait()
        oT[...] = oT[...] * alpha + dot(kv[zs, 1, rows, :].T, pst[zs, half], NN)

    mrow[...] = jnp.full(mrow.shape, NEG, F32)
    lrow[...] = jnp.zeros(lrow.shape, F32)
    oT[...] = jnp.zeros(oT.shape, F32)
    dqT[...] = jnp.zeros(dqT.shape, F32)
    for a in range(2):
        wz_in[1, a] = jnp.zeros((64, TOK), BF)

    def d_copies(e):
        src = dsend.at[:, pl.ds(e * HD, HD)]
        dst = dos.at[q_rows, :]
        far = remote(src, dst, d_send.at[e], d_recv.at[xr], dev(2 * c + e, z, y, xc))
        near = pltpu.make_async_copy(src, dst, d_recv.at[xr])
        return far, near

    def gx_copy(k):
        to = xplus(k)
        return remote(
            g_all.at[2 * to + c], gx.at[x, c], gx_send.at[0], gx_recv.at[k], dev(to, z, y, c)
        )

    def gx_forward(k):
        ref = gx.at[xplus(-k), c]
        return remote(ref, ref, gxf_send.at[0], gxf_recv.at[k], sibling)

    def chunk_of(t):
        return zplus(lax.div(t + 1, 2) * (1 - 2 * lax.rem(t, 2)))

    def forward_step(t, carry):
        dist = lax.div(t + 1, 2)
        zs = chunk_of(t)

        def arrival(e, dist):
            a, h = lax.rem(e, 2), lax.div(e, 2)
            for direction in range(2):
                r = h if direction == 0 else 1 - h
                src = zplus(dist * (2 * direction - 1))
                await_at(piece(src, a, r), ag_recv.at[direction, dist - 1, a, r])
                pl.when((dist < 3) | (h == 0))(ag_copy(direction, dist + 1, a, r, src).start)
                pl.when(a == 1)(sib_copy(2 * dist - 1 + direction, r, src).start)

        def slot(s):
            e = s + 1

            @pl.when((s > 2) & (s < 11))
            def _():
                arrival(lax.rem(e, 4), lax.div(e, 4) + 1)

        @pl.when(t == 0)
        def _():
            for a in range(2):
                for r in range(2):
                    await_at(piece(z, a, r), a_recv.at[r, a])
                    ag_copy(r, 1, a, r, z).start()
            for r in range(2):
                sib_copy(t, r, z).start()
            for a in range(2):
                for direction in range(2):
                    ag_copy(direction, 1, a, 1 - direction, z).start()
            for r in range(2):
                await_at(qs.at[pl.ds(r * TOK, TOK), :], a_recv.at[r, 2])

        @pl.when(t == 1)
        def _():
            for e in range(4):
                arrival(jnp.int32(e), jnp.int32(1))

        @pl.when(t == 7)
        def _():
            for r in range(2):
                await_at(piece(zs, 0, r), ag_recv.at[r, 3, 0, r])
            last_sib_copy(0, zs).start()

        slot(2 * t)

        @pl.when(t == 1)
        def _():
            for k in (1, 2, 3):
                await_at(g_all.at[y_slot(k, c)], y_recv.at[k])
                y_forward(k, g_all, yf_send, yf_recv).start()
            g_load.wait()
            w_load.wait()

        @pl.when(t == 2)
        def _():
            await_at(g_all.at[y * 2 + 1 - c], y_recv.at[0])
            for k in (1, 2, 3):
                await_at(g_all.at[y_slot(k, 1 - c)], yf_recv.at[k])
            d = jnp.zeros((TOK, TOK), F32)
            for h in range(8):
                d = d + dot(g_all[h], w_in[:, h * TOK:(h + 1) * TOK], NT)
            dsend[...] = d.astype(BF)
            for e in range(2):
                start_either(*d_copies(e), e)
            for k in range(1, NX):
                gx_copy(k).start()

        @pl.when(t == 3)
        def _():
            for k in range(1, 8):
                w_copy(k).start()
            for h in range(2):
                gx[x, h] = g_all[2 * x + h]
            w_all[j] = w_in[:, pl.ds(pl.multiple_of(j * TOK, TOK), TOK)]

        other_rows = pl.ds(pl.multiple_of((1 - c) * HALF, HALF), HALF)

        def values_here():
            @pl.when(t == 7)
            def _():
                for r in range(2):
                    await_at(piece(zs, 1, r), ag_recv.at[r, 3, 1, r])
                last_sib_copy(1, zs).start()

        def values_there():
            @pl.when(t == 7)
            def _():
                await_at(kv.at[zs, 1, other_rows, :], sib_recv.at[7, 1])

        forward_unit(zs, c, values_here)
        slot(2 * t + 1)

        @pl.when(t < 7)
        def _():
            for r in range(2):
                await_at(pair(zs, 1 - c, r), sib_recv.at[t, r])

        @pl.when(t == 7)
        def _():
            await_at(kv.at[zs, 0, other_rows, :], sib_recv.at[7, 0])

        forward_unit(zs, 1 - c, values_there)

        @pl.when(t == 6)
        def _():
            for r in range(2):
                await_at(dos.at[pl.ds(r * TOK, TOK), :], d_recv.at[r])
            dof[...] = dos[...].astype(F32).T

        return carry

    lax.fori_loop(0, 8, forward_step, 0)

    inv = 1.0 / lrow[...]
    attnT = (oT[...] * inv).astype(BF).astype(F32)
    aT[...] = attnT
    delta[...] = jnp.sum(dof[...] * attnT, axis=0, keepdims=True)

    def o_copies(k):
        dst = afull.at[c, :, pl.ds(pl.multiple_of(xr * HD, HD), HD)]
        far = remote(osend, dst, o_send.at[k], o_recv.at[xr, c], dev(xplus(k), z, y, xc))
        near = pltpu.make_async_copy(osend, dst, o_recv.at[xr, c])
        return far, near

    def sb_copy(u):
        return remote(sib_out.at[u], sib_in.at[u], sb_send.at[0], sb_recv.at[u], sibling)

    def sb_wait(u):
        await_at(sib_in.at[u], sb_recv.at[u])

    def rs_copy(direction, dist, a):
        return remote(
            rs_out.at[direction, dist - 1, a], rs_in.at[direction, dist - 1, a],
            rs_send.at[0 if dist == 4 else 1], rs_recv.at[direction, dist - 1, a],
            dev(x, zplus(1 - 2 * direction), y, c),
        )

    def g_copy(direction, r, a):
        return remote(
            rs_out.at[direction, 0, a, pl.ds(r * TOK, TOK), :], gkv.at[direction, xr, a],
            g_send.at[direction, r, a], g_recv.at[direction, xr, a],
            dev(2 * c + r, zplus(1 - 2 * direction), y, xc),
        )

    def total(u, a):
        return part[u, a] + sib_in[u, a].astype(F32)

    def ring(direction, dist, a):
        value = total(0 if dist == 4 else 7 - 2 * dist + direction, a)
        if dist < 3 or (dist == 3 and a == direction):
            await_at(rs_in.at[direction, dist, a], rs_recv.at[direction, dist, a])
            value = value + rs_in[direction, dist, a].astype(F32)
        rs_out[direction, dist - 1, a] = value.astype(BF)
        if dist > 1:
            rs_copy(direction, dist, a).start()
        else:
            for r in range(2):
                g_copy(direction, r, a).start()

    def wz_copy(kind, direction):
        src, dst = wz_out.at[kind, direction], wz_in.at[kind, direction]
        if kind == 1:
            rows = pl.ds(32 * direction, 32)
            src, dst = src.at[rows, :], dst.at[rows, :]
        far = (1, 2, 1, 2)[kind] * (1 - 2 * direction)
        return remote(
            src, dst, wz_send.at[0 if kind == 1 else 1], wz_recv.at[kind, direction],
            dev(x, zplus(far), y, c),
        )

    def wz_wait(kind, direction):
        dst = wz_in.at[kind, direction]
        if kind == 1:
            dst = dst.at[pl.ds(32 * direction, 32), :]
        await_at(dst, wz_recv.at[kind, direction])

    def wz_start():
        for kind in (1, 0, 2):
            for direction in range(2):
                to = zplus((3, 4, 1)[kind] * (1 - 2 * direction))
                wz_out[kind, direction] = wgp[to].astype(BF)
                wz_copy(kind, direction).start()

    def wz_middle():
        for direction in range(2):
            for kind in (1, 0):
                wz_wait(kind, direction)
            value = wgp[zplus(2 - 4 * direction)]
            value = value + wz_in[0, direction].astype(F32) + wz_in[1, direction].astype(F32)
            wz_out[3, direction] = value.astype(BF)
            wz_copy(3, direction).start()

    def backward_unit(zs, half):
        rows = pl.ds(pl.multiple_of(half * HALF, HALF), HALF)
        dk = dv = None
        for side in range(2):
            cols = slice(side * TOK, (side + 1) * TOK)
            factor = jnp.exp2((mst[zs, half, :, cols] - mrow[:, cols]) * EXP2_SCALE) / lrow[:, cols]
            p = pst[zs, half, :, cols].astype(F32) * factor
            dp = dot(kv[zs, 1, rows, :], dos[cols, :], NT)
            ds = (p * (dp - delta[:, cols])).astype(BF)
            dv_side = dot(p.astype(BF), dos[cols, :], NN)
            pst[zs, half, :, cols] = ds
            dk_side = dot(ds, qs[cols, :], NN)
            dk = dk_side if side == 0 else dk + dk_side
            dv = dv_side if side == 0 else dv + dv_side
        return dk * SCALE, dv

    def query_step(zs, carry):
        both = dot(kv[zs, 0, :HALF, :].T, pst[zs, 0], NN)
        dqT[...] += both + dot(kv[zs, 0, HALF:, :].T, pst[zs, 1], NN)
        return carry

    own_attn = afull.at[xc, q_rows, :]

    def f_copies(r, a):
        src = gsend.at[a, pl.ds(r * TOK, TOK), :]
        dst = gkv.at[2, xr, a] if a < 2 else gq.at[xr]
        far = remote(src, dst, f_send.at[r, a], f_recv.at[xr, a], dev(2 * c + r, z, y, xc))
        near = pltpu.make_async_copy(src, dst, f_recv.at[xr, a])
        return far, near

    def backward_step(n, carry):
        u = jnp.where(n == 5, 7, jnp.where(n > 5, n - 1, n))
        dist = lax.div(8 - u, 2)
        odd = lax.rem(u, 2)
        zs = zplus(dist * (2 * odd - 1))
        dk, dv = backward_unit(zs, 1 - c)
        sib_out[u, 0] = dk.astype(BF)
        sib_out[u, 1] = dv.astype(BF)
        sb_copy(u).start()
        dk, dv = backward_unit(zs, c)
        part[u, 0] = dk
        part[u, 1] = dv

        @pl.when(u == 0)
        def _():
            osend[...] = aT[...].T.astype(BF)
            for k in range(NX):
                far, near = o_copies(k)
                if k:
                    far.start()
                else:
                    pl.when(c != xc)(far.start)
                    pl.when(c == xc)(near.start)
            sb_wait(0)
            for a in range(2):
                ring(a, 4, a)

        @pl.when(u == 1)
        def _():
            sb_wait(1)
            ring(0, 3, 1)

        @pl.when(u == 2)
        def _():
            sb_wait(2)
            ring(1, 3, 0)
            for k in range(1, NX):
                await_at(gx.at[xplus(-k), c], gx_recv.at[k])
                gx_forward(k).start()

        @pl.when(u == 3)
        def _():
            for direction in range(2):
                ring(direction, 3, direction)

        @pl.when(u == 7)
        def _():
            sb_wait(3)
            sb_wait(4)
            for direction in range(2):
                ring(direction, 2, 1 - direction)
            sb_wait(7)
            for a in range(2):
                gsend[a] = total(7, a).astype(BF)
                for r in range(2):
                    start_either(*f_copies(r, a), r)
            for e in range(2):
                for half in range(2):
                    await_at(afull.at[half, :, pl.ds(e * HD, HD)], o_recv.at[e, half])
            for k in (1, 2, 3, 0):
                y_copies(k, own_attn, aall, ya_send, ya_recv).start()
            for k in range(1, NX):
                await_at(gx.at[xplus(-k), 1 - c], gxf_recv.at[k])
            for h in range(2):
                wg = jnp.zeros((TOK, TOK), F32)
                for xx in range(NX):
                    at = afull[xx // 2, (xx % 2) * TOK:(xx % 2 + 1) * TOK, :]
                    wg = wg + dot(gx[xx, h], at, TN)
                for n in range(4):
                    wgp[4 * h + n] = wg[n * 64:(n + 1) * 64, :]
            wz_start()
            aall[j] = own_attn[...]

        @pl.when(u == 5)
        def _():
            for direction in range(2):
                ring(direction, 2, direction)

        return carry

    lax.fori_loop(0, 8, backward_step, 0)

    lax.fori_loop(0, 4, query_step, 0)
    sb_wait(5)
    sb_wait(6)
    for direction in range(2):
        ring(direction, 1, 1 - direction)
    wz_middle()
    lax.fori_loop(4, 8, query_step, 0)
    gsend[2] = (dqT[...] * SCALE).T.astype(BF)
    for r in range(2):
        start_either(*f_copies(r, 2), r)
    for direction in range(2):
        ring(direction, 1, direction)
    for k in (1, 2, 3):
        await_at(aall.at[y_slot(k, c)], ya_recv.at[k])
        y_forward(k, aall, yaf_send, yaf_recv).start()

    for k in range(1, 8):
        w_wait(k)
    await_at(aall.at[y * 2 + 1 - c], ya_recv.at[0])
    for k in (1, 2, 3):
        await_at(aall.at[y_slot(k, 1 - c)], yaf_recv.at[k])
    o = jnp.zeros((TOK, TOK), F32)
    for h in range(8):
        o = o + dot(aall[h], w_all[h], NN)
    out_vm[...] = o.astype(BF)
    out_store = pltpu.make_async_copy(out_vm, out_ref, l_sem.at[2])
    out_store.start()

    for e in range(2):
        for a in range(3):
            far, _ = a_copies(e, a)
            pl.when(x != 2 * c + e)(far.wait_send)
            far, _ = f_copies(e, a)
            pl.when(x != 2 * c + e)(far.wait_send)
        far, _ = d_copies(e)
        pl.when(x != 2 * c + e)(far.wait_send)
    far, _ = o_copies(0)
    pl.when(c != xc)(far.wait_send)
    for k in range(1, NX):
        far, _ = o_copies(k)
        far.wait_send()

    def left(ref, sem):
        remote(ref, ref, sem, sem, sibling).wait_send()

    left(g_all.at[pl.ds(0, 4)], y_send.at[0])
    left(g_all.at[pl.ds(0, 4)], ya_send.at[0])
    for sem in (yf_send, yaf_send, gx_send, gxf_send):
        left(g_all.at[pl.ds(0, 3)], sem.at[0])
    left(w_all.at[pl.ds(0, 7)], w_send.at[0])
    left(sib_out, sb_send.at[0])
    left(kv.at[:, :, pl.ds(0, HALF), :], sib_send.at[0])
    left(rs_out.at[0, 3], rs_send.at[0])
    left(rs_out.at[:, pl.ds(1, 2)], rs_send.at[1])
    for direction in range(2):
        for dist in range(1, 4):
            left(kv.at[0, :, pl.ds(0, HALF), :], ag_send.at[direction, dist - 1])
        left(kv.at[0, 0, pl.ds(0, HALF), :], ag_send.at[direction, 3])

    wg = wgp[z]
    for kind in (2, 3):
        for direction in range(2):
            wz_wait(kind, direction)
            wg = wg + wz_in[kind, direction].astype(F32)
    wg_vm[...] = wg.astype(BF)
    wg_store = pltpu.make_async_copy(wg_vm, wg_ref, l_sem.at[3])
    wg_store.start()
    left(wz_out.at[0, 0], wz_send.at[0])
    left(wz_out.at[pl.ds(0, 3)], wz_send.at[1])

    for e in range(2):
        await_at(gq.at[e], f_recv.at[e, 2])
        for a in range(2):
            await_at(gkv.at[2, e, a], f_recv.at[e, a])
    out_store.wait()
    wg_store.wait()
    for direction in range(2):
        for r in range(2):
            for a in range(2):
                g_copy(direction, r, a).wait_send()
    for a in range(2):
        for e in range(2):
            for direction in range(2):
                await_at(gkv.at[direction, e, a], g_recv.at[direction, e, a])


def last_kernel(held_out, gq, gkv, held_wg, out_ref, dq_ref, dk_ref, dv_ref, wg_ref):
    out_ref[...] = held_out[...]
    wg_ref[...] = held_wg[...]
    for e in range(2):
        cols = slice(e * HD, (e + 1) * HD)
        dq_ref[:, cols] = gq[e]
        for a, ref in ((0, dk_ref), (1, dv_ref)):
            value = gkv[0, e, a].astype(F32) + gkv[1, e, a].astype(F32) + gkv[2, e, a].astype(F32)
            ref[:, cols] = value.astype(BF)


def on_device(queries, key_rows, value_rows, w_out, out_grad, tile_kind):
    vmem = pl.BlockSpec(memory_space=pltpu.VMEM)
    smem = pl.BlockSpec(memory_space=pltpu.SMEM)
    anywhere = pl.BlockSpec(memory_space=pl.ANY)
    V = pltpu.VMEM
    S = lambda *shape: pltpu.SemaphoreType.DMA(shape)
    scratch = [
        V((NZ, 2, 2 * HALF, HD), BF),
        V((HALF, HD), BF),
        V((HALF, HD), BF),
        V((NZ, 2, HALF, HALF), BF),
        V((NZ, 2, 1, HALF), F32),
        V((HD, HALF), F32),
        V((HD, HALF), F32),
        V((1, HALF), F32),
        V((1, HALF), F32),
        V((HD, HALF), F32),
        V((HD, HALF), F32),
        V((1, HALF), F32),
        V((TOK, 8 * TOK), BF),
        V((8, TOK, TOK), BF),
        V((8, TOK, TOK), BF),
        V((TOK, TOK), BF),
        V((NX, 2, TOK, TOK), BF),
        V((HALF, HD), BF),
        V((2, HALF, TOK), BF),
        V((8, TOK, TOK), BF),
        V((8, 2, HALF, HD), F32),
        V((8, 2, HALF, HD), BF),
        V((8, 2, HALF, HD), BF),
        V((2, 4, 2, HALF, HD), BF),
        V((2, 4, 2, HALF, HD), BF),
        V((NZ, 64, TOK), F32),
        V((4, 2, 64, TOK), BF),
        V((4, 2, 64, TOK), BF),
        V((3, HALF, HD), BF),
        V((TOK, TOK), BF),
        V((64, TOK), BF),
        S(4), S(2, 3), S(2, 3), S(2, 4), S(2, 4, 2, 2), S(1), S(8, 2),
        S(1), S(4), S(1), S(4), S(1), S(8), S(2), S(2),
        S(1), S(4), S(1), S(4),
        S(4), S(2, 2), S(1), S(4), S(1), S(4),
        S(2), S(2, 4, 2), S(1), S(8), S(2), S(4, 2), S(2, 3), S(2, 3),
        S(2, 2, 2), S(2, 2, 2),
    ]
    shape = lambda *s: jax.ShapeDtypeStruct(s, BF)
    outs = [shape(TOK, TOK)] * 4 + [shape(64, TOK)]
    held = pl.pallas_call(
        kernel,
        out_shape=[shape(TOK, TOK), shape(2, TOK, HD), shape(3, 2, 2, TOK, HD), shape(64, TOK)],
        in_specs=[anywhere] * 5 + [smem],
        out_specs=[anywhere] * 4,
        scratch_shapes=scratch,
        compiler_params=pltpu.CompilerParams(
            collective_id=0, has_side_effects=True, vmem_limit_bytes=56 * 1024 * 1024
        ),
        cost_estimate=pl.CostEstimate(flops=8 * 10**9, bytes_accessed=4 * 10**6, transcendentals=0),
    )(queries, key_rows, value_rows, w_out, out_grad, tile_kind)
    out, dq, dk, dv, wg = pl.pallas_call(
        last_kernel, out_shape=outs, in_specs=[vmem] * 4, out_specs=[vmem] * 5
    )(*held)
    return out, dq, dk, dv, wg.T


def solution(mesh):
    in_specs = (
        P("ctx", "head"),
        P("ctx", "head"),
        P("ctx", "head"),
        P("head", None),
        P("ctx", "head"),
        P(),
    )
    out_specs = (
        P("ctx", "head"),
        P("ctx", "head"),
        P("ctx", "head"),
        P("ctx", "head"),
        P("head", "ctx"),
    )
    return jax.shard_map(
        on_device, mesh=mesh, in_specs=in_specs, out_specs=out_specs, check_vma=False
    )
```
